32 devices in a mesh: groups: 2 (over y), row: 8 (over z, x), col: 2 (over core).
Axes of the slice: x: 2, y: 2, z: 4, core: 2. Of those that a mesh axis runs over, the one named last changes fastest.
Arguments:
- activations: bfloat16 [384, 14336], P(('groups', 'row', 'col')), parts along dimension 0, may hold values from -6 to 6
- pseudo_grads: bfloat16 [384, 4096], P(('groups', 'row', 'col')), parts along dimension 0, may hold values from -6 to 6
- row_counts: int32 [32], P(('groups', 'row', 'col')), parts along dimension 0, may hold values from 1 to 12, 144 in all
Outputs:
- act_cov: float32 [28672, 14336], P(('groups', 'row'), 'col'), parts along dimension 0
- grad_cov: float32 [8192, 4096], P(('groups', 'row'), 'col'), parts along dimension 0
The draws below stay inside these ranges and needn't reach their ends.
There are 2 independent parts, one for each index of `groups`. The reference program is written for one: setup_inputs(seed, part) draws one part's arguments, and reference() takes and returns one part's arrays. A program takes and returns all parts, laid end to end along the dimension named above; each array names one. Nothing has to cross between parts.
Inputs may be any that keep to these rules, and one draw needn't show every extreme that they name: `row_counts`: the counts sum to 144; some device holds exactly 12.
All inputs are finite; a program needn't handle non-finite values.
Results may differ from the reference program's by a relative error of at most 0.0003.
Values may be sent and summed in bfloat16 or wider, within the bound.
No kernel may reach another device: no remote copies, remote signals or barrier semaphores. Data moves between devices by JAX's collectives and lax.ppermute only.
A program may use at most 384 MiB of HBM per device.

```python
import math
import jax
import jax.numpy as jnp
import numpy as np
from jax import lax

D_IN = 14336
D_OUT = 4096
CAP = 12
TOKENS = 192
LIVE = 144
N_ROW = 8
N_COL = 2


def levels(key, dims, shards, low, top_value):
    factor_of, own = 1.0, jax.random.fold_in(key, 6)
    for axis_at, shards_of in shards:
        steps = jnp.exp(jax.random.uniform(jax.random.fold_in(own, axis_at), (shards_of,), jnp.float32, low / len(shards), top_value / len(shards)))
        factor_of = factor_of * jnp.repeat(steps, dims[axis_at] // shards_of).reshape([-1 if axis == axis_at else 1 for axis in range(len(dims))])
    return factor_of


def length_profile(amount, total, bound, lean):
    portions = [(1 << 20) // math.isqrt(standing ** lean) + 1 for standing in range(2, amount + 1)]
    spare, given = total - bound - (amount - 1), [1] * (amount - 1)
    while spare > 0:
        free = [i for i in range(amount - 1) if given[i] < bound]
        mass, left = sum([portions[i] for i in free]), spare
        for i in free:
            more = min(bound - given[i], max(1, left * portions[i] // mass), spare)
            given[i] = given[i] + more
            spare = spare - more
    return np.array([bound] + given)


def uneven(own_key, amount, total, most, lean):
    if amount == 2:
        one = jax.random.randint(own_key, (), max(1, total - most), min(most, total - 1) + 1)
        return jnp.stack([one, total - one])
    tallies = jnp.asarray(length_profile(amount, total, most, lean), jnp.int32)
    twos = (amount - 1) // 2
    source_of, taker = tallies[1:1 + 2 * twos:2], tallies[2:2 + 2 * twos:2]
    room = jnp.minimum(source_of - 1, most - taker)
    moved = jax.random.randint(jax.random.fold_in(own_key, 1), (twos,), 0, 1 << 20) % (room + 1)
    tallies = tallies.at[1:1 + 2 * twos:2].set(source_of - moved).at[2:2 + 2 * twos:2].set(taker + moved)
    return tallies[jax.random.permutation(jax.random.fold_in(own_key, 2), amount)]


def normal_values(rng, dims, deviation, reach, pieces=(), kind=jnp.bfloat16):
    factor_of = levels(rng, dims, pieces, -0.22, 0.18) if pieces else 1.0
    values = jax.random.normal(rng, dims, jnp.float32) * deviation * factor_of
    return jnp.minimum(jnp.maximum(values, -reach), reach).astype(kind)


def setup_inputs(seed: int = 0, part: int = 0) -> dict:
    arg_keys = jax.random.split(jax.random.key(seed), 4)
    part_keys = jax.random.split(jax.random.fold_in(arg_keys[3], part), 4)
    activations = normal_values(part_keys[0], (TOKENS, D_IN), 1.0, 6.0, ((0, 16),))
    pseudo_grads = normal_values(part_keys[1], (TOKENS, D_OUT), 1.0, 6.0, ((0, 16),))
    row_counts = uneven(part_keys[2], N_ROW * N_COL, LIVE, CAP, 1).astype(jnp.int32)
    return {"activations": activations, "pseudo_grads": pseudo_grads, "row_counts": row_counts}


def reference(activations, pseudo_grads, row_counts):
    position = jnp.arange(TOKENS, dtype=jnp.int32)
    owner = (position // CAP).astype(jnp.int32)
    live_mask = ((position % CAP) < row_counts[owner]).astype(jnp.float32)[:, None]
    live = jnp.sum(row_counts.astype(jnp.float32))
    act_full = activations.astype(jnp.float32)
    grad_full = pseudo_grads.astype(jnp.float32)
    act_cov = jnp.dot((act_full * live_mask).T, act_full, precision=lax.Precision.HIGHEST) / live
    grad_cov = jnp.dot((grad_full * live_mask).T, grad_full, precision=lax.Precision.HIGHEST) / live
    return act_cov, grad_cov
```

```python
import functools

import jax
import jax.numpy as jnp
from jax import lax
from jax.experimental import pallas as pl
from jax.experimental.pallas import tpu as pltpu
from jax.sharding import PartitionSpec as P


def chip_ring(rows):
    width = 2 if rows <= 8 else 4
    depth = rows // width
    order = [z * width for z in range(depth)]
    for step, z in enumerate(reversed(range(depth))):
        columns = range(1, width) if step % 2 == 0 else range(width - 1, 0, -1)
        order += [z * width + x for x in columns]
    return order


def gram_kernel(live, left_ref, *refs):
    right_refs, out_ref, turned = refs[:-2], refs[-2], refs[-1]

    @pl.when(pl.program_id(0) == 0)
    def _():
        turned[...] = left_ref[...].T

    right = jnp.concatenate([ref[...] for ref in right_refs], axis=0)
    out_ref[...] = jnp.dot(turned[...], right, preferred_element_type=jnp.float32) / live


def gram(left, rights, live, tile):
    tokens, height = left.shape
    width = rights[0].shape[1]
    return pl.pallas_call(
        functools.partial(gram_kernel, live),
        grid=(width // tile,),
        in_specs=[pl.BlockSpec((tokens, height), lambda j: (0, 0))]
        + [pl.BlockSpec((part.shape[0], tile), lambda j: (0, j)) for part in rights],
        out_specs=pl.BlockSpec((height, tile), lambda j: (0, j)),
        out_shape=jax.ShapeDtypeStruct((height, width), jnp.float32),
        scratch_shapes=[pltpu.VMEM((height, tokens), jnp.bfloat16)],
        compiler_params=pltpu.CompilerParams(vmem_limit_bytes=40 * 1024 * 1024),
        cost_estimate=pl.CostEstimate(
            flops=2 * tokens * height * width, bytes_accessed=4 * height * width, transcendentals=0
        ),
    )(left, *rights)


def solution(mesh):
    rows, cols = mesh.shape["row"], mesh.shape["col"]
    order = chip_ring(rows)
    ahead = [(order[p], order[(p + 1) % rows]) for p in range(rows)]
    behind = [(target, source) for source, target in ahead]
    swap = [(0, 1), (1, 0)]
    live = 9.0 * rows * cols

    def local(activations, pseudo_grads, row_counts):
        row, col = lax.axis_index("row"), lax.axis_index("col")
        slots, act_width = activations.shape
        grad_width = pseudo_grads.shape[1]
        act_half, grad_half = act_width // cols, grad_width // cols
        act_block, grad_block = act_width // rows, grad_width // rows
        position = jnp.arange(slots, dtype=jnp.int32)
        live_mask = (position < row_counts[0]).astype(jnp.bfloat16)[:, None]

        def pair_half(values, half):
            masked = values * live_mask
            mine = lax.dynamic_slice_in_dim(masked, col * half, half, 1)
            other = lax.ppermute(lax.dynamic_slice_in_dim(masked, (1 - col) * half, half, 1), "col", swap)
            first = jnp.where(col == 0, mine, other)
            second = jnp.where(col == 0, other, mine)
            return jnp.concatenate([first, second], axis=0)

        shards = [[pair_half(activations, act_half)], [pair_half(pseudo_grads, grad_half)]]
        forward = [shards[0][0], shards[1][0]]
        backward = list(forward)
        for _ in range(rows // 2 - 1):
            for k in (0, 1):
                forward[k] = lax.ppermute(forward[k], "row", ahead)
                backward[k] = lax.ppermute(backward[k], "row", behind)
                shards[k] += [forward[k], backward[k]]
        for k in (0, 1):
            middle = forward[k].shape[1] // 2
            shards[k].append(
                jnp.concatenate(
                    [
                        lax.ppermute(forward[k][:, :middle], "row", ahead),
                        lax.ppermute(backward[k][:, middle:], "row", behind),
                    ],
                    axis=1,
                )
            )
        half_rows = rows // cols
        outs = []
        for parts, block, tile in ((shards[0], act_block, 512), (shards[1], grad_block, 512)):
            here = (row % half_rows) * block
            own = [lax.dynamic_slice_in_dim(part, here, block, 1) for part in parts]
            early = len(parts) - 3
            groups = [jnp.concatenate(own[:early], axis=0), jnp.concatenate(own[early:], axis=0)]
            left = jnp.concatenate(
                [jnp.where(col == row // half_rows, g, lax.ppermute(g, "col", swap)) for g in groups], axis=0
            )
            outs.append(gram(left, parts, live, tile))
        return tuple(outs)

    return jax.shard_map(
        local,
        mesh=mesh,
        in_specs=(
            P(("groups", "row", "col"), None),
            P(("groups", "row", "col"), None),
            P(("groups", "row", "col")),
        ),
        out_specs=(P(("groups", "row"), "col"), P(("groups", "row"), "col")),
        check_vma=False,
    )
```

```python
import functools

import jax
import jax.numpy as jnp
from jax import lax
from jax.experimental import pallas as pl
from jax.experimental.pallas import tpu as pltpu
from jax.sharding import PartitionSpec as P


def chip_ring(rows):
    width = 2 if rows <= 8 else 4
    depth = rows // width
    order = [z * width for z in range(depth)]
    for step, z in enumerate(reversed(range(depth))):
        columns = range(1, width) if step % 2 == 0 else range(width - 1, 0, -1)
        order += [z * width + x for x in columns]
    return order


def gram_kernel(scale, shards, lists, pieces, left_ref, *refs):
    out_ref, turned, joined = refs[-3:]
    column, which, piece = pl.program_id(0), pl.program_id(1), pl.program_id(2)

    @pl.when((column == 0) & (which == 0) & (piece == 0))
    def _():
        turned[...] = left_ref[...].T

    for index in range(lists):

        @pl.when((which == index) & (piece == 0))
        def _(index=index):
            parts = refs[index * shards : (index + 1) * shards]
            joined[...] = jnp.concatenate([ref[...] for ref in parts], axis=0)

    height = out_ref.shape[0]
    if pieces == 1:
        rows = turned[...]
    else:
        rows = turned[pl.ds(pl.multiple_of(piece * height, height), height), :]
    out_ref[...] = jnp.dot(rows, joined[...], preferred_element_type=jnp.float32) * scale


def gram(left, right_lists, scale, out_shape, blocks, tile, pieces, out_index, out=None):
    tokens, height = left.shape
    shards, lists = len(right_lists[0]), len(right_lists)
    flat = [part for parts in right_lists for part in parts]
    in_specs = [pl.BlockSpec((tokens, height), lambda j, w, h: (0, 0))]
    in_specs += [pl.BlockSpec((part.shape[0], tile), lambda j, w, h: (0, j)) for part in flat]
    operands, aliases = [left, *flat], {}
    if out is not None:
        aliases = {len(operands): 0}
        in_specs.append(pl.BlockSpec(memory_space=pl.ANY))
        operands.append(out)
    work = tokens * height * blocks * lists * tile
    return pl.pallas_call(
        functools.partial(gram_kernel, scale, shards, lists, pieces),
        grid=(blocks, lists, pieces),
        in_specs=in_specs,
        out_specs=pl.BlockSpec((height // pieces, tile), out_index),
        out_shape=jax.ShapeDtypeStruct(out_shape, jnp.float32),
        scratch_shapes=[pltpu.VMEM((height, tokens), jnp.bfloat16), pltpu.VMEM((tokens, tile), jnp.bfloat16)],
        input_output_aliases=aliases,
        compiler_params=pltpu.CompilerParams(vmem_limit_bytes=40 * 1024 * 1024),
        cost_estimate=pl.CostEstimate(
            flops=2 * work, bytes_accessed=4 * work // tokens, transcendentals=0
        ),
    )(*operands)


def split_kernel(halves, order, half_ref, count_ref, act_ref, grad_ref, keep_ref, send_ref):
    live = lax.broadcasted_iota(jnp.int32, (act_ref.shape[0], 128), 0) < count_ref[0]
    for half in range(halves):
        for flip, out_ref in ((0, keep_ref), (1, send_ref)):

            @pl.when((half_ref[0] + flip) % halves == half)
            def _(half=half, out_ref=out_ref):
                for source, start, width, target in order:
                    ref = (grad_ref, act_ref)[source]
                    first = half * (ref.shape[1] // halves) + start
                    values = ref[:, first : first + width]
                    mask = jnp.concatenate([live] * (width // 128), axis=1)
                    out_ref[:, target : target + width] = jnp.where(mask, values, jnp.zeros_like(values))


def solution(mesh):
    rows, cols = mesh.shape["row"], mesh.shape["col"]
    order = chip_ring(rows)
    ahead = [(order[p], order[(p + 1) % rows]) for p in range(rows)]
    behind = [(target, source) for source, target in ahead]
    swap = [(0, 1), (1, 0)]
    half_rows = rows // cols
    scale = 1.0 / (9.0 * rows * cols)

    def local(activations, pseudo_grads, row_counts):
        row, col = lax.axis_index("row"), lax.axis_index("col")
        slots, act_width = activations.shape
        grad_width = pseudo_grads.shape[1]
        act_half, grad_half = act_width // cols, grad_width // cols
        act_block, grad_block = act_width // rows, grad_width // rows
        lists = 2 if act_block % 256 == 0 else 1
        sub = act_block // lists
        widths = [grad_half] + [act_half // lists] * lists
        offsets = [sum(widths[:k]) for k in range(len(widths))]

        layout = [(0, 0, grad_half, 0)]
        if lists == 1:
            layout.append((1, 0, act_half, offsets[1]))
        else:
            for k in range(lists):
                for j in range(half_rows):
                    layout.append((1, j * act_block + k * sub, sub, offsets[1 + k] + j * sub))
        half_shape = jax.ShapeDtypeStruct((slots, grad_half + act_half), jnp.bfloat16)
        keep, send = pl.pallas_call(
            functools.partial(split_kernel, cols, layout),
            in_specs=[pl.BlockSpec(memory_space=pltpu.SMEM)] * 2 + [pl.BlockSpec(memory_space=pltpu.VMEM)] * 2,
            out_specs=[pl.BlockSpec(memory_space=pltpu.VMEM)] * 2,
            out_shape=[half_shape, half_shape],
        )(col[None], row_counts, activations, pseudo_grads)
        other = lax.ppermute(send, "col", swap)
        first, second = jnp.where(col == 0, keep, other), jnp.where(col == 0, other, keep)

        chains = []
        for start, width in zip(offsets, widths):
            own = jnp.concatenate([first[:, start : start + width], second[:, start : start + width]], axis=0)
            chains.append([own])
        forward = [chain[0] for chain in chains]
        backward = list(forward)
        steps, halfway = [0] * len(chains), rows // 2
        sequence = [0, 1, 2, 0, 1, 0, 2, 1, 0, 2, 1, 2] if lists == 2 and halfway == 4 else list(range(len(chains))) * halfway
        previous = ()
        for k in sequence:
            chain, latest = chains[k], (forward[k], backward[k])
            (ahead_of, behind_of), _ = lax.optimization_barrier((latest, previous))
            previous = latest
            steps[k] += 1
            if steps[k] < halfway:
                forward[k] = lax.ppermute(ahead_of, "row", ahead)
                backward[k] = lax.ppermute(behind_of, "row", behind)
                chain += [forward[k], backward[k]]
            else:
                middle = widths[k] // 2
                upper = lax.ppermute(ahead_of[:, :middle], "row", ahead)
                lower = lax.ppermute(behind_of[:, middle:], "row", behind)
                chain.append(jnp.concatenate([upper, lower], axis=1))

        lefts = []
        for chain, block in zip(chains, [grad_block] + [sub] * lists):
            here = (row % half_rows) * block
            own = [lax.dynamic_slice_in_dim(part, here, block, 1) for part in chain]
            early = len(chain) - 3
            groups = [jnp.concatenate(own[:early], axis=0), jnp.concatenate(own[early:], axis=0)]
            lefts.append(
                jnp.concatenate(
                    [jnp.where(col == row // half_rows, g, lax.ppermute(g, "col", swap)) for g in groups], axis=0
                )
            )

        grad_tile = min(512, grad_half)
        grad_cov = gram(
            lefts[0], [chains[0]], scale, (grad_block, grad_half), grad_half // grad_tile, grad_tile, 1,
            lambda j, w, h: (0, j),
        )
        shape = (act_block, act_half)
        if lists == 1:
            act_cov = gram(lefts[1], [chains[1]], scale, shape, act_half // 256, 256, 1, lambda j, w, h: (0, j))
        else:
            act_cov = gram(
                lefts[1], [chains[1]], scale, shape, half_rows, sub, 2, lambda j, w, h: (h, 2 * j)
            )
            act_cov = gram(
                lefts[1], [chains[2]], scale, shape, half_rows, sub, 2, lambda j, w, h: (h, 2 * j + 1), act_cov
            )
            act_cov = gram(
                lefts[2], chains[1:], scale, shape, half_rows, sub, 2, lambda j, w, h: (2 + h, 2 * j + w), act_cov
            )
        return act_cov, grad_cov

    return jax.shard_map(
        local,
        mesh=mesh,
        in_specs=(
            P(("groups", "row", "col"), None),
            P(("groups", "row", "col"), None),
            P(("groups", "row", "col")),
        ),
        out_specs=(P(("groups", "row"), "col"), P(("groups", "row"), "col")),
        check_vma=False,
    )
```

```python
import functools

import jax
import jax.numpy as jnp
from jax import lax
from jax.experimental import pallas as pl
from jax.experimental.pallas import tpu as pltpu
from jax.sharding import PartitionSpec as P


SLOTS = 4


def chip_ring(rows):
    width = 2 if rows <= 8 else 4
    depth = rows // width
    order = [z * width for z in range(depth)]
    for step, z in enumerate(reversed(range(depth))):
        columns = range(1, width) if step % 2 == 0 else range(width - 1, 0, -1)
        order += [z * width + x for x in columns]
    return order


def gram_kernel(scale, left_ref, *refs):
    right_refs, out_ref, turned = refs[:-2], refs[-2], refs[-1]

    @pl.when(pl.program_id(0) == 0)
    def _():
        turned[...] = left_ref[...].T

    right = jnp.concatenate([ref[...] for ref in right_refs], axis=0)
    out_ref[...] = jnp.dot(turned[...], right, preferred_element_type=jnp.float32) * scale


def gram(left, rights, scale, steps, tile):
    tokens, height = left.shape
    return pl.pallas_call(
        functools.partial(gram_kernel, scale),
        grid=(steps,),
        in_specs=[pl.BlockSpec((tokens, height), lambda j: (0, 0))]
        + [pl.BlockSpec((part.shape[0], tile), lambda j: (0, j)) for part in rights],
        out_specs=pl.BlockSpec((height, tile), lambda j: (0, j)),
        out_shape=jax.ShapeDtypeStruct((height, steps * tile), jnp.float32),
        scratch_shapes=[pltpu.VMEM((height, tokens), jnp.bfloat16)],
        compiler_params=pltpu.CompilerParams(vmem_limit_bytes=32 * 1024 * 1024),
    )(left, *rights)


def tiles_kernel(scale, groups, lefts, lists, outs, aliased, *refs):
    left_refs, refs = refs[:lefts], refs[lefts:]
    sources = []
    for shards in lists:
        sources.append(refs[:shards])
        refs = refs[shards:]
    out_refs = refs[aliased : aliased + outs]
    turned, buffer, sems = refs[aliased + outs : -2], refs[-2], refs[-1]
    for left_ref, turned_ref in zip(left_refs, turned):
        turned_ref[...] = left_ref[...].T

    def copy(group, slot, j):
        _, _, _, _, height, width, which, row, column, stride, _ = group
        return pltpu.make_async_copy(
            buffer.at[slot, pl.ds(0, height), pl.ds(0, width)],
            out_refs[which].at[pl.ds(row, height), pl.ds(pl.multiple_of(column + j * stride, 128), width)],
            sems.at[slot],
        )

    earlier = None
    for group in groups:

        def step(j, carry, group=group, earlier=earlier):
            left, source, first, apart, height, width, _, _, _, _, _ = group
            slot = lax.rem(j, SLOTS)

            @pl.when(j >= SLOTS)
            def _():
                copy(group, slot, j - SLOTS).wait()

            if earlier is not None:

                @pl.when(j < SLOTS)
                def _():
                    copy(earlier, slot, j + earlier[-1] - SLOTS).wait()

            here = pl.ds(pl.multiple_of(first + j * apart, 128), width)
            right = jnp.concatenate([ref[:, here] for ref in sources[source]], axis=0)
            product = jnp.dot(turned[left][...], right, preferred_element_type=jnp.float32)
            buffer[slot, :height, :width] = product * scale
            copy(group, slot, j).start()
            return carry

        lax.fori_loop(0, group[-1], step, 0)
        earlier = group
    for slot in range(SLOTS):
        copy(earlier, slot, earlier[-1] - SLOTS + slot).wait()


def tiles(scale, groups, lefts, lists, out_shapes, out=None):
    tokens = lefts[0].shape[0]
    whole, anywhere = pl.BlockSpec(memory_space=pltpu.VMEM), pl.BlockSpec(memory_space=pl.ANY)
    operands = [*lefts, *[part for parts in lists for part in parts]]
    specs, aliases = [whole] * len(operands), {}
    if out is not None:
        aliases = {len(operands): 0}
        operands.append(out)
        specs.append(anywhere)
    area = sum(g[4] * g[5] * g[10] for g in groups)
    return pl.pallas_call(
        functools.partial(
            tiles_kernel, scale, groups, len(lefts), [len(parts) for parts in lists], len(out_shapes), len(aliases)
        ),
        in_specs=specs,
        out_specs=[anywhere] * len(out_shapes),
        out_shape=[jax.ShapeDtypeStruct(shape, jnp.float32) for shape in out_shapes],
        scratch_shapes=[pltpu.VMEM((left.shape[1], tokens), jnp.bfloat16) for left in lefts]
        + [
            pltpu.VMEM((SLOTS, max(g[4] for g in groups), max(g[5] for g in groups)), jnp.float32),
            pltpu.SemaphoreType.DMA((SLOTS,)),
        ],
        input_output_aliases=aliases,
        compiler_params=pltpu.CompilerParams(vmem_limit_bytes=32 * 1024 * 1024),
        cost_estimate=pl.CostEstimate(flops=2 * tokens * area, bytes_accessed=4 * area, transcendentals=0),
    )(*operands)


def split_kernel(halves, order, half_ref, count_ref, act_ref, grad_ref, keep_ref, send_ref):
    live = lax.broadcasted_iota(jnp.int32, (act_ref.shape[0], 128), 0) < count_ref[0]
    for half in range(halves):
        for flip, out_ref in ((0, keep_ref), (1, send_ref)):

            @pl.when((half_ref[0] + flip) % halves == half)
            def _(half=half, out_ref=out_ref):
                for source, start, width, target in order:
                    ref = (grad_ref, act_ref)[source]
                    first = half * (ref.shape[1] // halves) + start
                    values = ref[:, first : first + width]
                    mask = jnp.concatenate([live] * (width // 128), axis=1)
                    out_ref[:, target : target + width] = jnp.where(mask, values, jnp.zeros_like(values))


def solution(mesh):
    rows, cols = mesh.shape["row"], mesh.shape["col"]
    order = chip_ring(rows)
    ahead = [(order[p], order[(p + 1) % rows]) for p in range(rows)]
    behind = [(target, source) for source, target in ahead]
    swap = [(0, 1), (1, 0)]
    half_rows = rows // cols
    scale = 1.0 / (9.0 * rows * cols)

    def local(activations, pseudo_grads, row_counts):
        row, col = lax.axis_index("row"), lax.axis_index("col")
        slots, act_width = activations.shape
        grad_width = pseudo_grads.shape[1]
        act_half, grad_half = act_width // cols, grad_width // cols
        act_block, grad_block = act_width // rows, grad_width // rows
        cut = act_block * 4 // 7 if act_block % 1792 == 0 else act_block
        rest = act_block - cut
        widths = [half_rows * cut, half_rows * rest + grad_half]
        layout = [(1, j * act_block, cut, j * cut) for j in range(half_rows)]
        if rest == 0:
            layout = [(1, 0, act_half, 0)]
        else:
            layout += [(1, j * act_block + cut, rest, widths[0] + j * rest) for j in range(half_rows)]
        layout.append((0, 0, grad_half, widths[0] + half_rows * rest))
        half_shape = jax.ShapeDtypeStruct((slots, grad_half + act_half), jnp.bfloat16)
        keep, send = pl.pallas_call(
            functools.partial(split_kernel, cols, layout),
            in_specs=[pl.BlockSpec(memory_space=pltpu.SMEM)] * 2 + [pl.BlockSpec(memory_space=pltpu.VMEM)] * 2,
            out_specs=[pl.BlockSpec(memory_space=pltpu.VMEM)] * 2,
            out_shape=[half_shape, half_shape],
        )(col[None], row_counts, activations, pseudo_grads)
        other = lax.ppermute(send, "col", swap)
        first, second = jnp.where(col == 0, keep, other), jnp.where(col == 0, other, keep)

        chains = []
        for start, width in ((0, widths[0]), (widths[0], widths[1])):
            own = jnp.concatenate([first[:, start : start + width], second[:, start : start + width]], axis=0)
            chains.append([own])
        forward = [chain[0] for chain in chains]
        backward = list(forward)
        steps, halfway = [0] * len(chains), rows // 2
        sequence = [0, 1] * halfway
        previous = ()
        for k in sequence:
            chain, latest = chains[k], (forward[k], backward[k])
            (ahead_of, behind_of), _ = lax.optimization_barrier((latest, previous))
            previous = latest
            steps[k] += 1
            if steps[k] < halfway:
                forward[k] = lax.ppermute(ahead_of, "row", ahead)
                backward[k] = lax.ppermute(behind_of, "row", behind)
                chain += [forward[k], backward[k]]
            else:
                middle = widths[k] // 2
                upper = lax.ppermute(ahead_of[:, :middle], "row", ahead)
                lower = lax.ppermute(behind_of[:, middle:], "row", behind)
                chain.append(jnp.concatenate([upper, lower], axis=1))

        def left_part(chain, pieces):
            own = []
            for part in chain:
                cuts = [
                    lax.dynamic_slice_in_dim(part, base + (row % half_rows) * size, size, 1) for base, size in pieces
                ]
                own.append(cuts[0] if len(cuts) == 1 else jnp.concatenate(cuts, axis=1))
            early = len(own) - 3
            groups = [jnp.concatenate(own[:early], axis=0), jnp.concatenate(own[early:], axis=0)]
            mine = col == row // half_rows
            return jnp.concatenate([jnp.where(mine, g, lax.ppermute(g, "col", swap)) for g in groups], axis=0)

        act_shape, grad_shape = (act_block, act_half), (grad_block, grad_half)
        left_first = left_part(chains[0], [(0, cut)])
        if rest == 0:
            left_grad = left_part(chains[1], [(0, grad_block)])
            act_cov = gram(left_first, chains[0], scale, act_half // 256, 256)
            grad_cov = gram(left_grad, chains[1], scale, grad_half // 256, 256)
        else:
            grad_first = half_rows * rest
            left_second = left_part(chains[1], [(0, rest), (grad_first, grad_block)])
            half_cut = cut // 2
            (act_cov,) = tiles(
                scale,
                [
                    (0, 0, part * half_cut, cut, cut, half_cut, 0, 0, part * half_cut, act_block, half_rows)
                    for part in (0, 1)
                ],
                [left_first], [chains[0]], [act_shape],
            )
            lefts = [left_first, left_second[:, :rest], left_second[:, rest:]]
            act_cov, grad_cov = tiles(
                scale,
                [
                    (0, 1, 0, rest, cut, rest, 0, 0, cut, act_block, half_rows),
                    (1, 0, 0, cut, rest, cut, 0, cut, 0, act_block, half_rows),
                    (1, 1, 0, rest, rest, rest, 0, cut, cut, act_block, half_rows),
                    (2, 1, grad_first, grad_block, grad_block, grad_block, 1, 0, 0, grad_block, half_rows),
                ],
                lefts, chains, [act_shape, grad_shape], act_cov,
            )
        return act_cov, grad_cov

    return jax.shard_map(
        local,
        mesh=mesh,
        in_specs=(
            P(("groups", "row", "col"), None),
            P(("groups", "row", "col"), None),
            P(("groups", "row", "col")),
        ),
        out_specs=(P(("groups", "row"), "col"), P(("groups", "row"), "col")),
        check_vma=False,
    )
```

```python
import functools

import jax
import jax.numpy as jnp
from jax import lax
from jax.experimental import pallas as pl
from jax.experimental.pallas import tpu as pltpu
from jax.sharding import PartitionSpec as P


SLOTS, COPIES = 4, 2


def chip_ring(rows):
    width = 2 if rows <= 8 else 4
    depth = rows // width
    order = [z * width for z in range(depth)]
    for step, z in enumerate(reversed(range(depth))):
        columns = range(1, width) if step % 2 == 0 else range(width - 1, 0, -1)
        order += [z * width + x for x in columns]
    return order


def gram_kernel(scale, left_ref, *refs):
    right_refs, out_ref, turned = refs[:-2], refs[-2], refs[-1]

    @pl.when(pl.program_id(0) == 0)
    def _():
        turned[...] = left_ref[...].T

    right = jnp.concatenate([ref[...] for ref in right_refs], axis=0)
    out_ref[...] = jnp.dot(turned[...], right, preferred_element_type=jnp.float32) * scale


def gram(left, rights, scale, steps, tile):
    tokens, height = left.shape
    return pl.pallas_call(
        functools.partial(gram_kernel, scale),
        grid=(steps,),
        in_specs=[pl.BlockSpec((tokens, height), lambda j: (0, 0))]
        + [pl.BlockSpec((part.shape[0], tile), lambda j: (0, j)) for part in rights],
        out_specs=pl.BlockSpec((height, tile), lambda j: (0, j)),
        out_shape=jax.ShapeDtypeStruct((height, steps * tile), jnp.float32),
        scratch_shapes=[pltpu.VMEM((height, tokens), jnp.bfloat16)],
        compiler_params=pltpu.CompilerParams(vmem_limit_bytes=32 * 1024 * 1024),
    )(left, *rights)


def tiles_kernel(scale, groups, lefts, lists, outs, aliased, *refs):
    left_refs, refs = refs[:lefts], refs[lefts:]
    sources = []
    for shards in lists:
        sources.append(refs[:shards])
        refs = refs[shards:]
    out_refs = refs[aliased : aliased + outs]
    turned, buffer, sems = refs[aliased + outs : -2], refs[-2], refs[-1]

    def copy(group, slot, j, start=0, rows=None):
        _, _, _, _, height, width, which, row, column, stride, _ = group
        rows = rows or height
        return pltpu.make_async_copy(
            buffer.at[slot, pl.ds(start, rows), pl.ds(0, width)],
            out_refs[which].at[pl.ds(row + start, rows), pl.ds(pl.multiple_of(column + j * stride, 128), width)],
            sems.at[slot],
        )

    earlier, ready = None, set()
    for group in groups:
        if group[0] not in ready:
            ready.add(group[0])
            turned[group[0]][...] = left_refs[group[0]][...].T

        def step(j, carry, group=group, earlier=earlier):
            left, source, first, apart, height, width, _, _, _, _, _ = group
            slot = lax.rem(j, SLOTS)

            @pl.when(j >= SLOTS)
            def _():
                copy(group, slot, j - SLOTS).wait()

            if earlier is not None:

                @pl.when(j < SLOTS)
                def _():
                    copy(earlier, slot, j + earlier[-1] - SLOTS).wait()

            here = pl.ds(pl.multiple_of(first + j * apart, 128), width)
            right = jnp.concatenate([ref[:, here] for ref in sources[source]], axis=0)
            product = jnp.dot(turned[left][...], right, preferred_element_type=jnp.float32)
            buffer[slot, :height, :width] = product * scale
            for start in range(0, height, height // COPIES):
                copy(group, slot, j, start, height // COPIES).start()
            return carry

        lax.fori_loop(0, group[-1], step, 0)
        earlier = group
    for slot in range(SLOTS):
        copy(earlier, slot, earlier[-1] - SLOTS + slot).wait()


def tiles(scale, groups, lefts, lists, out_shapes, out=None):
    tokens = lefts[0].shape[0]
    whole, anywhere = pl.BlockSpec(memory_space=pltpu.VMEM), pl.BlockSpec(memory_space=pl.ANY)
    operands = [*lefts, *[part for parts in lists for part in parts]]
    specs, aliases = [whole] * len(operands), {}
    if out is not None:
        aliases = {len(operands): 0}
        operands.append(out)
        specs.append(anywhere)
    area = sum(g[4] * g[5] * g[10] for g in groups)
    return pl.pallas_call(
        functools.partial(
            tiles_kernel, scale, groups, len(lefts), [len(parts) for parts in lists], len(out_shapes), len(aliases)
        ),
        in_specs=specs,
        out_specs=[anywhere] * len(out_shapes),
        out_shape=[jax.ShapeDtypeStruct(shape, jnp.float32) for shape in out_shapes],
        scratch_shapes=[pltpu.VMEM((left.shape[1], tokens), jnp.bfloat16) for left in lefts]
        + [
            pltpu.VMEM((SLOTS, max(g[4] for g in groups), max(g[5] for g in groups)), jnp.float32),
            pltpu.SemaphoreType.DMA((SLOTS,)),
        ],
        input_output_aliases=aliases,
        compiler_params=pltpu.CompilerParams(vmem_limit_bytes=32 * 1024 * 1024),
        cost_estimate=pl.CostEstimate(flops=2 * tokens * area, bytes_accessed=4 * area, transcendentals=0),
    )(*operands)


def split_kernel(halves, layouts, half_ref, count_ref, act_ref, grad_ref, *out_refs):
    slots = act_ref.shape[0]
    live = lax.broadcasted_iota(jnp.int32, (slots, 128), 0) < count_ref[0]
    for half in range(halves):
        for flip in (1, 0):

            @pl.when((half_ref[0] + flip) % halves == half)
            def _(half=half, flip=flip):
                for chain, layout in enumerate(layouts):
                    target = 0
                    for source, start, width in layout:
                        ref = (grad_ref, act_ref)[source]
                        first = half * (ref.shape[1] // halves) + start
                        values = ref[:, first : first + width]
                        mask = jnp.concatenate([live] * (width // 128), axis=1)
                        masked = jnp.where(mask, values, jnp.zeros_like(values))
                        own = (half + flip) % halves * slots
                        out_ref, columns = out_refs[2 * chain + flip], slice(target, target + width)
                        out_ref[own : own + slots, columns] = masked
                        other = slots - own
                        out_ref[other : other + slots, columns] = jnp.zeros_like(values)
                        target += width


def solution(mesh):
    rows, cols = mesh.shape["row"], mesh.shape["col"]
    order = chip_ring(rows)
    ahead = [(order[p], order[(p + 1) % rows]) for p in range(rows)]
    behind = [(target, source) for source, target in ahead]
    swap = [(0, 1), (1, 0)]
    half_rows = rows // cols
    scale = 1.0 / (9.0 * rows * cols)

    def local(activations, pseudo_grads, row_counts):
        row, col = lax.axis_index("row"), lax.axis_index("col")
        slots, act_width = activations.shape
        grad_width = pseudo_grads.shape[1]
        act_half, grad_half = act_width // cols, grad_width // cols
        act_block, grad_block = act_width // rows, grad_width // rows
        cut = act_block * 4 // 7 if act_block % 1792 == 0 else act_block
        rest = act_block - cut
        widths = [half_rows * cut, half_rows * rest + grad_half]
        if rest == 0:
            layouts = [[(1, 0, act_half)], [(0, 0, grad_half)]]
        else:
            layouts = [
                [(1, j * act_block, cut) for j in range(half_rows)],
                [(1, j * act_block + cut, rest) for j in range(half_rows)] + [(0, 0, grad_half)],
            ]
        pieces = pl.pallas_call(
            functools.partial(split_kernel, cols, layouts),
            in_specs=[pl.BlockSpec(memory_space=pltpu.SMEM)] * 2 + [pl.BlockSpec(memory_space=pltpu.VMEM)] * 2,
            out_specs=[pl.BlockSpec(memory_space=pltpu.VMEM)] * 4,
            out_shape=[jax.ShapeDtypeStruct((2 * slots, width), jnp.bfloat16) for width in widths for _ in (0, 1)],
        )(col[None], row_counts, activations, pseudo_grads)
        chains = [[pieces[2 * k] + lax.ppermute(pieces[2 * k + 1], "col", swap)] for k in (0, 1)]
        forward = [chain[0] for chain in chains]
        backward = list(forward)
        steps, halfway = [0] * len(chains), rows // 2
        sequence = [0, 1] * halfway
        previous, last = (), []
        for k in sequence:
            chain, latest = chains[k], (forward[k], backward[k])
            (ahead_of, behind_of), _ = lax.optimization_barrier((latest, previous))
            previous = latest
            steps[k] += 1
            if steps[k] < halfway:
                forward[k] = lax.ppermute(ahead_of, "row", ahead)
                backward[k] = lax.ppermute(behind_of, "row", behind)
                chain += [forward[k], backward[k]]
            else:
                middle = widths[k] // 2
                upper = lax.ppermute(ahead_of[:, :middle], "row", ahead)
                lower = lax.ppermute(behind_of[:, middle:], "row", behind)
                last.append((upper, lower))

        def left_part(chain, pieces):
            own = []
            for part in chain:
                cuts = [
                    lax.dynamic_slice_in_dim(part, base + (row % half_rows) * size, size, 1) for base, size in pieces
                ]
                own.append(cuts[0] if len(cuts) == 1 else jnp.concatenate(cuts, axis=1))
            early = len(own) - 3
            groups = [jnp.concatenate(own[:early], axis=0), jnp.concatenate(own[early:], axis=0)]
            mine = col == row // half_rows
            return jnp.concatenate([jnp.where(mine, g, lax.ppermute(g, "col", swap)) for g in groups], axis=0)

        act_shape, grad_shape = (act_block, act_half), (grad_block, grad_half)
        last_first, _ = lax.optimization_barrier((last[0], (forward[1], backward[1])))
        chains[0].append(jnp.concatenate(last_first, axis=1))
        left_first = left_part(chains[0], [(0, cut)])
        if rest == 0:
            chains[1].append(jnp.concatenate(last[1], axis=1))
            left_grad = left_part(chains[1], [(0, grad_block)])
            act_cov = gram(left_first, chains[0], scale, act_half // 256, 256)
            grad_cov = gram(left_grad, chains[1], scale, grad_half // 256, 256)
        else:
            tile, grad_first = cut // 4, half_rows * rest

            def square(part, out):
                group_of = lambda start: (0, 0, start, cut, cut, tile, 0, 0, start, act_block, half_rows)
                groups = [group_of(part * cut // 2), group_of(part * cut // 2 + tile)]
                return tiles(scale, groups, [left_first], [chains[0]], [act_shape], out)[0]

            act_cov = square(0, None)
            last_second, act_cov = lax.optimization_barrier((last[1], act_cov))
            chains[1].append(jnp.concatenate(last_second, axis=1))
            left_second = left_part(chains[1], [(0, rest), (grad_first, grad_block)])
            act_cov = square(1, act_cov)
            lefts = [left_first, left_second[:, :rest], left_second[:, rest:]]
            act_cov, grad_cov = tiles(
                scale,
                [
                    (0, 1, 0, rest, cut, rest, 0, 0, cut, act_block, half_rows),
                    (1, 0, 0, cut, rest, cut, 0, cut, 0, act_block, half_rows),
                    (1, 1, 0, rest, rest, rest, 0, cut, cut, act_block, half_rows),
                    (2, 1, grad_first, grad_block, grad_block, grad_block, 1, 0, 0, grad_block, half_rows),
                ],
                lefts, chains, [act_shape, grad_shape], act_cov,
            )
        return act_cov, grad_cov

    return jax.shard_map(
        local,
        mesh=mesh,
        in_specs=(
            P(("groups", "row", "col"), None),
            P(("groups", "row", "col"), None),
            P(("groups", "row", "col")),
        ),
        out_specs=(P(("groups", "row"), "col"), P(("groups", "row"), "col")),
        check_vma=False,
    )
```

```python
import functools

import jax
import jax.numpy as jnp
from jax import lax
from jax.experimental import pallas as pl
from jax.experimental.pallas import tpu as pltpu
from jax.sharding import PartitionSpec as P


SLOTS, COPIES = 4, 2


def chip_ring(rows):
    width = 2 if rows <= 8 else 4
    depth = rows // width
    order = [z * width for z in range(depth)]
    for step, z in enumerate(reversed(range(depth))):
        columns = range(1, width) if step % 2 == 0 else range(width - 1, 0, -1)
        order += [z * width + x for x in columns]
    return order


def gram_kernel(scale, left_ref, *refs):
    right_refs, out_ref, turned = refs[:-2], refs[-2], refs[-1]

    @pl.when(pl.program_id(0) == 0)
    def _():
        turned[...] = left_ref[...].T

    right = jnp.concatenate([ref[...] for ref in right_refs], axis=0)
    out_ref[...] = jnp.dot(turned[...], right, preferred_element_type=jnp.float32) * scale


def gram(left, rights, scale, steps, tile):
    tokens, height = left.shape
    return pl.pallas_call(
        functools.partial(gram_kernel, scale),
        grid=(steps,),
        in_specs=[pl.BlockSpec((tokens, height), lambda j: (0, 0))]
        + [pl.BlockSpec((part.shape[0], tile), lambda j: (0, j)) for part in rights],
        out_specs=pl.BlockSpec((height, tile), lambda j: (0, j)),
        out_shape=jax.ShapeDtypeStruct((height, steps * tile), jnp.float32),
        scratch_shapes=[pltpu.VMEM((height, tokens), jnp.bfloat16)],
        compiler_params=pltpu.CompilerParams(vmem_limit_bytes=32 * 1024 * 1024),
    )(left, *rights)


def tiles_kernel(scale, groups, lefts, lists, outs, aliased, *refs):
    left_refs, refs = refs[:lefts], refs[lefts:]
    sources = []
    for shards in lists:
        sources.append(refs[:shards])
        refs = refs[shards:]
    out_refs = refs[aliased : aliased + outs]
    turned, buffer, sems = refs[aliased + outs : -2], refs[-2], refs[-1]

    def copy(group, slot, j, start=0, rows=None):
        _, _, _, _, height, width, which, row, column, stride, _ = group
        rows = rows or height
        return pltpu.make_async_copy(
            buffer.at[slot, pl.ds(start, rows), pl.ds(0, width)],
            out_refs[which].at[pl.ds(row + start, rows), pl.ds(pl.multiple_of(column + j * stride, 128), width)],
            sems.at[slot],
        )

    earlier, ready = None, set()
    for group in groups:
        if group[0] not in ready:
            ready.add(group[0])
            turned[group[0]][...] = left_refs[group[0]][...].T

        def step(j, carry, group=group, earlier=earlier):
            left, source, first, apart, height, width, _, _, _, _, _ = group
            slot = lax.rem(j, SLOTS)

            @pl.when(j >= SLOTS)
            def _():
                copy(group, slot, j - SLOTS).wait()

            if earlier is not None:

                @pl.when(j < SLOTS)
                def _():
                    copy(earlier, slot, j + earlier[-1] - SLOTS).wait()

            here = pl.ds(pl.multiple_of(first + j * apart, 128), width)
            right = jnp.concatenate([ref[:, here] for ref in sources[source]], axis=0)
            product = jnp.dot(turned[left][...], right, preferred_element_type=jnp.float32)
            buffer[slot, :height, :width] = product * scale
            for start in range(0, height, height // COPIES):
                copy(group, slot, j, start, height // COPIES).start()
            return carry

        lax.fori_loop(0, group[-1], step, 0)
        earlier = group
    for slot in range(SLOTS):
        copy(earlier, slot, earlier[-1] - SLOTS + slot).wait()


def tiles(scale, groups, lefts, lists, out_shapes, out=None):
    tokens = lefts[0].shape[0]
    whole, anywhere = pl.BlockSpec(memory_space=pltpu.VMEM), pl.BlockSpec(memory_space=pl.ANY)
    operands = [*lefts, *[part for parts in lists for part in parts]]
    specs, aliases = [whole] * len(operands), {}
    if out is not None:
        aliases = {len(operands): 0}
        operands.append(out)
        specs.append(anywhere)
    area = sum(g[4] * g[5] * g[10] for g in groups)
    return pl.pallas_call(
        functools.partial(
            tiles_kernel, scale, groups, len(lefts), [len(parts) for parts in lists], len(out_shapes), len(aliases)
        ),
        in_specs=specs,
        out_specs=[anywhere] * len(out_shapes),
        out_shape=[jax.ShapeDtypeStruct(shape, jnp.float32) for shape in out_shapes],
        scratch_shapes=[pltpu.VMEM((left.shape[1], tokens), jnp.bfloat16) for left in lefts]
        + [
            pltpu.VMEM((SLOTS, max(g[4] for g in groups), max(g[5] for g in groups)), jnp.float32),
            pltpu.SemaphoreType.DMA((SLOTS,)),
        ],
        input_output_aliases=aliases,
        compiler_params=pltpu.CompilerParams(vmem_limit_bytes=32 * 1024 * 1024),
        cost_estimate=pl.CostEstimate(flops=2 * tokens * area, bytes_accessed=4 * area, transcendentals=0),
    )(*operands)


def split_kernel(halves, layouts, half_ref, count_ref, act_ref, grad_ref, *out_refs):
    slots = act_ref.shape[0]
    live = lax.broadcasted_iota(jnp.int32, (slots, 128), 0) < count_ref[0]
    for half in range(halves):
        for flip in (1, 0):

            @pl.when((half_ref[0] + flip) % halves == half)
            def _(half=half, flip=flip):
                for chain, layout in enumerate(layouts):
                    target = 0
                    for source, start, width in layout:
                        ref = (grad_ref, act_ref)[source]
                        first = half * (ref.shape[1] // halves) + start
                        values = ref[:, first : first + width]
                        mask = jnp.concatenate([live] * (width // 128), axis=1)
                        masked = jnp.where(mask, values, jnp.zeros_like(values))
                        own = (half + flip) % halves * slots
                        out_ref, columns = out_refs[2 * chain + flip], slice(target, target + width)
                        out_ref[own : own + slots, columns] = masked
                        other = slots - own
                        out_ref[other : other + slots, columns] = jnp.zeros_like(values)
                        target += width


def solution(mesh):
    rows, cols = mesh.shape["row"], mesh.shape["col"]
    order = chip_ring(rows)
    ahead = [(order[p], order[(p + 1) % rows]) for p in range(rows)]
    behind = [(target, source) for source, target in ahead]
    swap = [(0, 1), (1, 0)]
    half_rows = rows // cols
    scale = 1.0 / (9.0 * rows * cols)

    def local(activations, pseudo_grads, row_counts):
        row, col = lax.axis_index("row"), lax.axis_index("col")
        slots, act_width = activations.shape
        grad_width = pseudo_grads.shape[1]
        act_half, grad_half = act_width // cols, grad_width // cols
        act_block, grad_block = act_width // rows, grad_width // rows
        cut = act_block * 4 // 7 if act_block % 1792 == 0 else act_block
        rest = act_block - cut
        widths = [half_rows * cut, half_rows * rest + grad_half]
        if rest == 0:
            layouts = [[(1, 0, act_half)], [(0, 0, grad_half)]]
        else:
            layouts = [
                [(1, j * act_block, cut) for j in range(half_rows)],
                [(1, j * act_block + cut, rest) for j in range(half_rows)] + [(0, 0, grad_half)],
            ]
        pieces = pl.pallas_call(
            functools.partial(split_kernel, cols, layouts),
            in_specs=[pl.BlockSpec(memory_space=pltpu.SMEM)] * 2 + [pl.BlockSpec(memory_space=pltpu.VMEM)] * 2,
            out_specs=[pl.BlockSpec(memory_space=pltpu.VMEM)] * 4,
            out_shape=[pltpu.VMEM((2 * slots, width), jnp.bfloat16) for width in widths for _ in (0, 1)],
        )(col[None], row_counts, activations, pseudo_grads)
        chains = [[pieces[2 * k] + lax.ppermute(pieces[2 * k + 1], "col", swap)] for k in (0, 1)]
        forward = [chain[0] for chain in chains]
        backward = list(forward)
        steps, halfway = [0] * len(chains), rows // 2
        sequence = [0, 1] * halfway
        previous, last = (), []
        for k in sequence:
            chain, middle = chains[k], widths[k] // 2
            steps[k] += 1
            final = steps[k] == halfway
            ahead_of, _ = lax.optimization_barrier((forward[k], previous))
            behind_of, _ = lax.optimization_barrier((backward[k], previous))
            previous = forward[k]
            if final:
                ahead_of, behind_of = ahead_of[:, :middle], behind_of[:, middle:]
            forward[k] = lax.ppermute(ahead_of, "row", ahead)
            backward[k] = lax.ppermute(behind_of, "row", behind)
            if final:
                last.append((forward[k], backward[k]))
            else:
                chain += [forward[k], backward[k]]
                latest = (forward[k], backward[k])

        def left_part(chain, pieces):
            own = []
            for part in chain:
                cuts = [
                    lax.dynamic_slice_in_dim(part, base + (row % half_rows) * size, size, 1) for base, size in pieces
                ]
                own.append(cuts[0] if len(cuts) == 1 else jnp.concatenate(cuts, axis=1))
            early = len(own) - 3
            groups = [jnp.concatenate(own[:early], axis=0), jnp.concatenate(own[early:], axis=0)]
            mine = col == row // half_rows
            return jnp.concatenate([jnp.where(mine, g, lax.ppermute(g, "col", swap)) for g in groups], axis=0)

        act_shape, grad_shape = (act_block, act_half), (grad_block, grad_half)
        last_first, _ = lax.optimization_barrier((last[0], latest))
        chains[0].append(jnp.concatenate(last_first, axis=1))
        left_first = left_part(chains[0], [(0, cut)])
        if rest == 0:
            chains[1].append(jnp.concatenate(last[1], axis=1))
            left_grad = left_part(chains[1], [(0, grad_block)])
            act_cov = gram(left_first, chains[0], scale, act_half // 256, 256)
            grad_cov = gram(left_grad, chains[1], scale, grad_half // 256, 256)
        else:
            tile, grad_first = cut // 4, half_rows * rest

            def square(part, out):
                group_of = lambda start: (0, 0, start, cut, cut, tile, 0, 0, start, act_block, half_rows)
                groups = [group_of(part * cut // 2), group_of(part * cut // 2 + tile)]
                return tiles(scale, groups, [left_first], [chains[0]], [act_shape], out)[0]

            act_cov = square(0, None)
            last_second, act_cov = lax.optimization_barrier((last[1], act_cov))
            chains[1].append(jnp.concatenate(last_second, axis=1))
            left_second = left_part(chains[1], [(0, rest), (grad_first, grad_block)])
            act_cov = square(1, act_cov)
            lefts = [left_first, left_second[:, :rest], left_second[:, rest:]]
            act_cov, grad_cov = tiles(
                scale,
                [
                    (0, 1, 0, rest, cut, rest, 0, 0, cut, act_block, half_rows),
                    (1, 0, 0, cut, rest, cut, 0, cut, 0, act_block, half_rows),
                    (1, 1, 0, rest, rest, rest, 0, cut, cut, act_block, half_rows),
                    (2, 1, grad_first, grad_block, grad_block, grad_block, 1, 0, 0, grad_block, half_rows),
                ],
                lefts, chains, [act_shape, grad_shape], act_cov,
            )
        return act_cov, grad_cov

    return jax.shard_map(
        local,
        mesh=mesh,
        in_specs=(
            P(("groups", "row", "col"), None),
            P(("groups", "row", "col"), None),
            P(("groups", "row", "col")),
        ),
        out_specs=(P(("groups", "row"), "col"), P(("groups", "row"), "col")),
        check_vma=False,
    )
```

```python
import functools

import jax
import jax.numpy as jnp
from jax import lax
from jax.experimental import pallas as pl
from jax.experimental.pallas import tpu as pltpu
from jax.sharding import PartitionSpec as P


SLOTS, COPIES = 4, 2


def chip_ring(rows):
    width = 2 if rows <= 8 else 4
    depth = rows // width
    order = [z * width for z in range(depth)]
    for step, z in enumerate(reversed(range(depth))):
        columns = range(1, width) if step % 2 == 0 else range(width - 1, 0, -1)
        order += [z * width + x for x in columns]
    return order


def gram_kernel(scale, left_ref, *refs):
    right_refs, out_ref, turned = refs[:-2], refs[-2], refs[-1]

    @pl.when(pl.program_id(0) == 0)
    def _():
        turned[...] = left_ref[...].T

    right = jnp.concatenate([ref[...] for ref in right_refs], axis=0)
    out_ref[...] = jnp.dot(turned[...], right, preferred_element_type=jnp.float32) * scale


def gram(left, rights, scale, steps, tile):
    tokens, height = left.shape
    return pl.pallas_call(
        functools.partial(gram_kernel, scale),
        grid=(steps,),
        in_specs=[pl.BlockSpec((tokens, height), lambda j: (0, 0))]
        + [pl.BlockSpec((part.shape[0], tile), lambda j: (0, j)) for part in rights],
        out_specs=pl.BlockSpec((height, tile), lambda j: (0, j)),
        out_shape=jax.ShapeDtypeStruct((height, steps * tile), jnp.float32),
        scratch_shapes=[pltpu.VMEM((height, tokens), jnp.bfloat16)],
        compiler_params=pltpu.CompilerParams(vmem_limit_bytes=32 * 1024 * 1024),
    )(left, *rights)


def tiles_kernel(scale, groups, lefts, lists, outs, aliased, *refs):
    left_refs, refs = refs[:lefts], refs[lefts:]
    sources = []
    for shards in lists:
        sources.append(refs[:shards])
        refs = refs[shards:]
    out_refs = refs[aliased : aliased + outs]
    turned, buffer, sems = refs[aliased + outs : -2], refs[-2], refs[-1]

    def copy(group, slot, j, start=0, rows=None):
        _, _, _, _, height, width, which, row, column, stride, _ = group
        rows = rows or height
        return pltpu.make_async_copy(
            buffer.at[slot, pl.ds(start, rows), pl.ds(0, width)],
            out_refs[which].at[pl.ds(row + start, rows), pl.ds(pl.multiple_of(column + j * stride, 128), width)],
            sems.at[slot],
        )

    earlier, ready = None, set()
    for group in groups:
        if group[0] not in ready:
            ready.add(group[0])
            turned[group[0]][...] = left_refs[group[0]][...].T

        def step(j, carry, group=group, earlier=earlier):
            left, source, first, apart, height, width, _, _, _, _, _ = group
            slot = lax.rem(j, SLOTS)

            @pl.when(j >= SLOTS)
            def _():
                copy(group, slot, j - SLOTS).wait()

            if earlier is not None:

                @pl.when(j < SLOTS)
                def _():
                    copy(earlier, slot, j + earlier[-1] - SLOTS).wait()

            here = pl.ds(pl.multiple_of(first + j * apart, 128), width)
            right = jnp.concatenate([ref[:, here] for ref in sources[source]], axis=0)
            product = jnp.dot(turned[left][...], right, preferred_element_type=jnp.float32)
            buffer[slot, :height, :width] = product * scale
            for start in range(0, height, height // COPIES):
                copy(group, slot, j, start, height // COPIES).start()
            return carry

        lax.fori_loop(0, group[-1], step, 0)
        earlier = group
    for slot in range(SLOTS):
        copy(earlier, slot, earlier[-1] - SLOTS + slot).wait()


def tiles(scale, groups, lefts, lists, out_shapes, out=None):
    tokens = lefts[0].shape[0]
    whole, anywhere = pl.BlockSpec(memory_space=pltpu.VMEM), pl.BlockSpec(memory_space=pl.ANY)
    operands = [*lefts, *[part for parts in lists for part in parts]]
    specs, aliases = [whole] * len(operands), {}
    if out is not None:
        aliases = {len(operands): 0}
        operands.append(out)
        specs.append(anywhere)
    area = sum(g[4] * g[5] * g[10] for g in groups)
    return pl.pallas_call(
        functools.partial(
            tiles_kernel, scale, groups, len(lefts), [len(parts) for parts in lists], len(out_shapes), len(aliases)
        ),
        in_specs=specs,
        out_specs=[anywhere] * len(out_shapes),
        out_shape=[jax.ShapeDtypeStruct(shape, jnp.float32) for shape in out_shapes],
        scratch_shapes=[pltpu.VMEM((left.shape[1], tokens), jnp.bfloat16) for left in lefts]
        + [
            pltpu.VMEM((SLOTS, max(g[4] for g in groups), max(g[5] for g in groups)), jnp.float32),
            pltpu.SemaphoreType.DMA((SLOTS,)),
        ],
        input_output_aliases=aliases,
        compiler_params=pltpu.CompilerParams(vmem_limit_bytes=32 * 1024 * 1024),
        cost_estimate=pl.CostEstimate(flops=2 * tokens * area, bytes_accessed=4 * area, transcendentals=0),
    )(*operands)


def split_kernel(halves, layouts, half_ref, count_ref, act_ref, grad_ref, *out_refs):
    slots = act_ref.shape[0]
    live = lax.broadcasted_iota(jnp.int32, (slots, 128), 0) < count_ref[0]
    for half in range(halves):
        for flip in (1, 0):

            @pl.when((half_ref[0] + flip) % halves == half)
            def _(half=half, flip=flip):
                for chain, layout in enumerate(layouts):
                    target = 0
                    for source, start, width in layout:
                        ref = (grad_ref, act_ref)[source]
                        first = half * (ref.shape[1] // halves) + start
                        values = ref[:, first : first + width]
                        mask = jnp.concatenate([live] * (width // 128), axis=1)
                        masked = jnp.where(mask, values, jnp.zeros_like(values))
                        own = (half + flip) % halves * slots
                        out_ref, columns = out_refs[2 * chain + flip], slice(target, target + width)
                        out_ref[own : own + slots, columns] = masked
                        other = slots - own
                        out_ref[other : other + slots, columns] = jnp.zeros_like(values)
                        target += width


def solution(mesh):
    rows, cols = mesh.shape["row"], mesh.shape["col"]
    order = chip_ring(rows)
    ahead = [(order[p], order[(p + 1) % rows]) for p in range(rows)]
    behind = [(target, source) for source, target in ahead]
    swap = [(0, 1), (1, 0)]
    half_rows = rows // cols
    scale = 1.0 / (9.0 * rows * cols)

    def local(activations, pseudo_grads, row_counts):
        row, col = lax.axis_index("row"), lax.axis_index("col")
        slots, act_width = activations.shape
        grad_width = pseudo_grads.shape[1]
        act_half, grad_half = act_width // cols, grad_width // cols
        act_block, grad_block = act_width // rows, grad_width // rows
        cut = act_block * 4 // 7 if act_block % 1792 == 0 else act_block
        rest = act_block - cut
        widths = [half_rows * cut, half_rows * rest + grad_half]
        if rest == 0:
            layouts = [[(1, 0, act_half)], [(0, 0, grad_half)]]
        else:
            layouts = [
                [(1, j * act_block, cut) for j in range(half_rows)],
                [(1, j * act_block + cut, rest) for j in range(half_rows)] + [(0, 0, grad_half)],
            ]
        pieces = pl.pallas_call(
            functools.partial(split_kernel, cols, layouts),
            in_specs=[pl.BlockSpec(memory_space=pltpu.SMEM)] * 2 + [pl.BlockSpec(memory_space=pltpu.VMEM)] * 2,
            out_specs=[pl.BlockSpec(memory_space=pltpu.VMEM)] * 4,
            out_shape=[pltpu.VMEM((2 * slots, width), jnp.bfloat16) for width in widths for _ in (0, 1)],
        )(col[None], row_counts, activations, pseudo_grads)
        chains = [[pieces[2 * k] + lax.ppermute(pieces[2 * k + 1], "col", swap)] for k in (0, 1)]
        forward = [chain[0] for chain in chains]
        backward = list(forward)
        steps, halfway = [0] * len(chains), rows // 2
        sequence = [0, 1] * halfway
        def left_part(chain, pieces, hold=None):
            own = []
            for part in chain:
                cuts = [
                    lax.dynamic_slice_in_dim(part, base + (row % half_rows) * size, size, 1) for base, size in pieces
                ]
                own.append(cuts[0] if len(cuts) == 1 else jnp.concatenate(cuts, axis=1))
            groups = [jnp.concatenate(own[:-1], axis=0), own[-1]]
            mine = col == row // half_rows
            if hold is not None:
                hold.append(groups[1])
            return jnp.concatenate([jnp.where(mine, g, lax.ppermute(g, "col", swap)) for g in groups], axis=0)

        previous, hold, left_first = (), [], None
        for k in sequence:
            chain, middle = chains[k], widths[k] // 2
            steps[k] += 1
            final = steps[k] == halfway
            ahead_of, _ = lax.optimization_barrier((forward[k], previous))
            behind_of, _ = lax.optimization_barrier((backward[k], (previous, hold)))
            previous = forward[k]
            if final:
                ahead_of, behind_of = ahead_of[:, :middle], behind_of[:, middle:]
            forward[k] = lax.ppermute(ahead_of, "row", ahead)
            backward[k] = lax.ppermute(behind_of, "row", behind)
            if not final:
                chain += [forward[k], backward[k]]
                latest = (forward[k], backward[k])
            elif k == 0:
                last_first, _ = lax.optimization_barrier(((forward[k], backward[k]), latest))
                chain.append(jnp.concatenate(last_first, axis=1))
                left_first = left_part(chain, [(0, cut)], hold)

        act_shape, grad_shape = (act_block, act_half), (grad_block, grad_half)
        if rest == 0:
            chains[1].append(jnp.concatenate((forward[1], backward[1]), axis=1))
            left_grad = left_part(chains[1], [(0, grad_block)])
            act_cov = gram(left_first, chains[0], scale, act_half // 256, 256)
            grad_cov = gram(left_grad, chains[1], scale, grad_half // 256, 256)
        else:
            grad_first = half_rows * rest

            def group(left, source, base, apart, height, start, width):
                row_at, column_at = left * cut, source * cut + start
                return (left, source, base + start, apart, height, width, 0, row_at, column_at, act_block, half_rows)

            def square(part, out):
                widths_of = (128, 256, 128) if cut == 1024 else (cut // 2,)
                starts = [part * cut // 2 + sum(widths_of[:n]) for n in range(len(widths_of))]
                groups = [group(0, 0, 0, cut, cut, start, width) for start, width in zip(starts, widths_of)]
                return tiles(scale, groups, [left_first], [chains[0]], [act_shape], out)[0]

            act_cov = square(0, None)
            last_second, act_cov = lax.optimization_barrier(((forward[1], backward[1]), act_cov))
            chains[1].append(jnp.concatenate(last_second, axis=1))
            left_second = left_part(chains[1], [(0, rest), (grad_first, grad_block)])
            act_cov = square(1, act_cov)
            lefts = [left_first, left_second[:, :rest], left_second[:, rest:]]
            act_cov, grad_cov = tiles(
                scale,
                [
                    (2, 1, grad_first, grad_block, grad_block, grad_block, 1, 0, 0, grad_block, half_rows),
                    group(0, 1, 0, rest, cut, 0, rest),
                    group(1, 0, 0, cut, rest, 0, cut),
                    *[group(1, 1, 0, rest, rest, start, rest // 3) for start in range(0, rest, rest // 3)],
                ],
                lefts, chains, [act_shape, grad_shape], act_cov,
            )
        return act_cov, grad_cov

    return jax.shard_map(
        local,
        mesh=mesh,
        in_specs=(
            P(("groups", "row", "col"), None),
            P(("groups", "row", "col"), None),
            P(("groups", "row", "col")),
        ),
        out_specs=(P(("groups", "row"), "col"), P(("groups", "row"), "col")),
        check_vma=False,
    )
```

```python
import functools

import jax
import jax.numpy as jnp
from jax import lax
from jax.experimental import pallas as pl
from jax.experimental.pallas import tpu as pltpu
from jax.sharding import PartitionSpec as P


SLOTS, HEIGHT = 4, 256


def chip_ring(rows):
    width = 2 if rows <= 8 else 4
    depth = rows // width
    order = [z * width for z in range(depth)]
    for step, z in enumerate(reversed(range(depth))):
        columns = range(1, width) if step % 2 == 0 else range(width - 1, 0, -1)
        order += [z * width + x for x in columns]
    return order


def gram_kernel(scale, left_ref, *refs):
    right_refs, out_ref, turned = refs[:-2], refs[-2], refs[-1]

    @pl.when(pl.program_id(0) == 0)
    def _():
        turned[...] = left_ref[...].T

    right = jnp.concatenate([ref[...] for ref in right_refs], axis=0)
    out_ref[...] = jnp.dot(turned[...], right, preferred_element_type=jnp.float32) * scale


def gram(left, rights, scale, steps, tile):
    tokens, height = left.shape
    return pl.pallas_call(
        functools.partial(gram_kernel, scale),
        grid=(steps,),
        in_specs=[pl.BlockSpec((tokens, height), lambda j: (0, 0))]
        + [pl.BlockSpec((part.shape[0], tile), lambda j: (0, j)) for part in rights],
        out_specs=pl.BlockSpec((height, tile), lambda j: (0, j)),
        out_shape=jax.ShapeDtypeStruct((height, steps * tile), jnp.float32),
        scratch_shapes=[pltpu.VMEM((height, tokens), jnp.bfloat16)],
        compiler_params=pltpu.CompilerParams(vmem_limit_bytes=32 * 1024 * 1024),
    )(left, *rights)


def tiles_kernel(scale, groups, ready, lists, outs, aliased, *refs):
    left_refs, refs = refs[: len(ready)], refs[len(ready) :]
    sources = []
    for shards in lists:
        sources.append(refs[:shards])
        refs = refs[shards:]
    refs = refs[aliased:]
    out_refs, turned = refs[:outs], list(refs[outs:-3])
    joined, buffer, sems = refs[-3:]
    turned = [left_ref if done else turned.pop(0) for left_ref, done in zip(left_refs, ready)]

    def copy(group, slot, j, m):
        _, height, _, width, which, row, column, stride, _, _ = group
        return pltpu.make_async_copy(
            buffer.at[slot, pl.ds(0, height), pl.ds(0, width)],
            out_refs[which].at[
                pl.ds(pl.multiple_of(row + m * height, 8), height),
                pl.ds(pl.multiple_of(column + j * stride, 128), width),
            ],
            sems.at[slot],
        )

    earlier, done = None, [index for index, is_ready in enumerate(ready) if is_ready]
    for group in groups:
        left, height, parts, width, _, _, _, _, blocks, pieces = group
        if left not in done:
            done.append(left)
            turned[left][...] = left_refs[left][...].T

        def step(n, carry, group=group, earlier=earlier):
            left, height, parts, width, _, _, _, _, blocks, pieces = group
            slot, j, m = lax.rem(n, SLOTS), lax.div(n, pieces), lax.rem(n, pieces)

            @pl.when(m == 0)
            def _():
                at = 0
                for source, first, apart, wide in parts:
                    here = pl.ds(pl.multiple_of(first + j * apart, 128), wide)
                    joined[:, at : at + wide] = jnp.concatenate([ref[:, here] for ref in sources[source]], axis=0)
                    at += wide

            @pl.when(n >= SLOTS)
            def _():
                copy(group, slot, 0, 0).wait()

            if earlier is not None:

                @pl.when(n < SLOTS)
                def _():
                    copy(earlier, slot, 0, 0).wait()

            rows = turned[left][pl.ds(pl.multiple_of(m * height, height), height), :]
            product = jnp.dot(rows, joined[:, :width], preferred_element_type=jnp.float32)
            buffer[slot, :height, :width] = product * scale
            copy(group, slot, j, m).start()
            return carry

        lax.fori_loop(0, blocks * pieces, step, 0)
        earlier = group
    for slot in range(SLOTS):
        copy(earlier, slot, 0, 0).wait()


def tiles(scale, groups, lefts, lists, out_shapes, out=None, ready=(), hand_on=False):
    ready = tuple(ready) or (False,) * len(lefts)
    tokens = lists[0][0].shape[0] * len(lists[0])
    whole, anywhere = pl.BlockSpec(memory_space=pltpu.VMEM), pl.BlockSpec(memory_space=pl.ANY)
    operands = [*lefts, *[part for parts in lists for part in parts]]
    specs, aliases = [whole] * len(operands), {}
    if out is not None:
        aliases = {len(operands): 0}
        operands.append(out)
        specs.append(anywhere)
    area = sum(g[1] * g[3] * g[8] * g[9] for g in groups)
    turned = [(left.shape[1], tokens) for left, done in zip(lefts, ready) if not done]
    results = [jax.ShapeDtypeStruct(shape, jnp.float32) for shape in out_shapes]
    result_specs = [anywhere] * len(results)
    if hand_on:
        results.append(pltpu.VMEM(turned[0], jnp.bfloat16))
        result_specs.append(whole)
    return pl.pallas_call(
        functools.partial(
            tiles_kernel, scale, groups, ready, [len(parts) for parts in lists], len(out_shapes), len(aliases)
        ),
        in_specs=specs,
        out_specs=result_specs,
        out_shape=results,
        scratch_shapes=[pltpu.VMEM(shape, jnp.bfloat16) for shape in turned[int(hand_on) :]]
        + [
            pltpu.VMEM((tokens, max(g[3] for g in groups)), jnp.bfloat16),
            pltpu.VMEM((SLOTS, max(g[1] for g in groups), max(g[3] for g in groups)), jnp.float32),
            pltpu.SemaphoreType.DMA((SLOTS,)),
        ],
        input_output_aliases=aliases,
        compiler_params=pltpu.CompilerParams(vmem_limit_bytes=32 * 1024 * 1024),
        cost_estimate=pl.CostEstimate(flops=2 * tokens * area, bytes_accessed=4 * area, transcendentals=0),
    )(*operands)


def split_kernel(halves, layouts, half_ref, count_ref, act_ref, grad_ref, *out_refs):
    slots = act_ref.shape[0]
    live = lax.broadcasted_iota(jnp.int32, (slots, 128), 0) < count_ref[0]
    for half in range(halves):
        for flip in (1, 0):

            @pl.when((half_ref[0] + flip) % halves == half)
            def _(half=half, flip=flip):
                for chain, layout in enumerate(layouts):
                    target = 0
                    for source, start, width in layout:
                        ref = (grad_ref, act_ref)[source]
                        first = half * (ref.shape[1] // halves) + start
                        values = ref[:, first : first + width]
                        mask = jnp.concatenate([live] * (width // 128), axis=1)
                        masked = jnp.where(mask, values, jnp.zeros_like(values))
                        own = (half + flip) % halves * slots
                        out_ref, columns = out_refs[2 * chain + flip], slice(target, target + width)
                        out_ref[own : own + slots, columns] = masked
                        other = slots - own
                        out_ref[other : other + slots, columns] = jnp.zeros_like(values)
                        target += width


def solution(mesh):
    rows, cols = mesh.shape["row"], mesh.shape["col"]
    order = chip_ring(rows)
    ahead = [(order[p], order[(p + 1) % rows]) for p in range(rows)]
    behind = [(target, source) for source, target in ahead]
    swap = [(0, 1), (1, 0)]
    half_rows = rows // cols
    scale = 1.0 / (9.0 * rows * cols)

    def local(activations, pseudo_grads, row_counts):
        row, col = lax.axis_index("row"), lax.axis_index("col")
        slots, act_width = activations.shape
        grad_width = pseudo_grads.shape[1]
        act_half, grad_half = act_width // cols, grad_width // cols
        act_block, grad_block = act_width // rows, grad_width // rows
        cut = act_block * 4 // 7 if act_block % 1792 == 0 else act_block
        rest = act_block - cut
        widths = [half_rows * cut, half_rows * rest + grad_half]
        if rest == 0:
            layouts = [[(1, 0, act_half)], [(0, 0, grad_half)]]
        else:
            layouts = [
                [(1, j * act_block, cut) for j in range(half_rows)],
                [(1, j * act_block + cut, rest) for j in range(half_rows)] + [(0, 0, grad_half)],
            ]
        pieces = pl.pallas_call(
            functools.partial(split_kernel, cols, layouts),
            in_specs=[pl.BlockSpec(memory_space=pltpu.SMEM)] * 2 + [pl.BlockSpec(memory_space=pltpu.VMEM)] * 2,
            out_specs=[pl.BlockSpec(memory_space=pltpu.VMEM)] * 4,
            out_shape=[pltpu.VMEM((2 * slots, width), jnp.bfloat16) for width in widths for _ in (0, 1)],
        )(col[None], row_counts, activations, pseudo_grads)
        chains = [[pieces[2 * k] + lax.ppermute(pieces[2 * k + 1], "col", swap)] for k in (0, 1)]
        forward = [chain[0] for chain in chains]
        backward = list(forward)
        steps, halfway = [0] * len(chains), rows // 2
        sequence = [0, 1] * halfway
        def left_part(chain, pieces, hold=None):
            own = []
            for part in chain:
                cuts = [
                    lax.dynamic_slice_in_dim(part, base + (row % half_rows) * size, size, 1) for base, size in pieces
                ]
                own.append(cuts[0] if len(cuts) == 1 else jnp.concatenate(cuts, axis=1))
            groups = [jnp.concatenate(own[:-1], axis=0), own[-1]]
            mine = col == row // half_rows
            if hold is not None:
                hold.append(groups[1])
            return jnp.concatenate([jnp.where(mine, g, lax.ppermute(g, "col", swap)) for g in groups], axis=0)

        previous, hold, left_first = (), [], None
        for k in sequence:
            chain, middle = chains[k], widths[k] // 2
            steps[k] += 1
            final = steps[k] == halfway
            ahead_of, _ = lax.optimization_barrier((forward[k], previous))
            behind_of, _ = lax.optimization_barrier((backward[k], (previous, hold)))
            previous = forward[k]
            if final:
                ahead_of, behind_of = ahead_of[:, :middle], behind_of[:, middle:]
            forward[k] = lax.ppermute(ahead_of, "row", ahead)
            backward[k] = lax.ppermute(behind_of, "row", behind)
            if not final:
                chain += [forward[k], backward[k]]
                latest = (forward[k], backward[k])
            elif k == 0:
                last_first, _ = lax.optimization_barrier(((forward[k], backward[k]), latest))
                chain.append(jnp.concatenate(last_first, axis=1))
                left_first = left_part(chain, [(0, cut)], hold)

        act_shape, grad_shape = (act_block, act_half), (grad_block, grad_half)
        if rest == 0:
            chains[1].append(jnp.concatenate((forward[1], backward[1]), axis=1))
            left_grad = left_part(chains[1], [(0, grad_block)])
            act_cov = gram(left_first, chains[0], scale, act_half // 256, 256)
            grad_cov = gram(left_grad, chains[1], scale, grad_half // 256, 256)
        else:
            grad_first = half_rows * rest
            first_part, second_part = (0, 0, cut, cut), (1, 0, rest, rest)
            grad_part = (1, grad_first, grad_block, grad_block)

            def square(part, lefts, out, **more):
                blocks = half_rows // 2
                start = part * blocks
                parts = [(0, start * cut, cut, cut)]
                group = (0, HEIGHT, parts, cut, 0, 0, start * act_block, act_block, blocks, cut // HEIGHT)
                return tiles(scale, [group], lefts, [chains[0]], [act_shape], out, **more)

            act_cov, turned_first = square(0, [left_first], None, hand_on=True)
            last_second, act_cov = lax.optimization_barrier(((forward[1], backward[1]), act_cov))
            chains[1].append(jnp.concatenate(last_second, axis=1))
            left_second = left_part(chains[1], [(0, rest), (grad_first, grad_block)])
            (act_cov,) = square(1, [turned_first], act_cov, ready=[True])
            act_cov, grad_cov = tiles(
                scale,
                [
                    (2, HEIGHT, [grad_part], grad_block, 1, 0, 0, grad_block, half_rows, grad_block // HEIGHT),
                    (1, HEIGHT, [first_part, second_part], act_block, 0, cut, 0, act_block, half_rows, rest // HEIGHT),
                    (0, HEIGHT, [second_part], rest, 0, 0, cut, act_block, half_rows, cut // HEIGHT),
                ],
                [turned_first, left_second[:, :rest], left_second[:, rest:]],
                chains, [act_shape, grad_shape], act_cov, ready=[True, False, False],
            )
        return act_cov, grad_cov

    return jax.shard_map(
        local,
        mesh=mesh,
        in_specs=(
            P(("groups", "row", "col"), None),
            P(("groups", "row", "col"), None),
            P(("groups", "row", "col")),
        ),
        out_specs=(P(("groups", "row"), "col"), P(("groups", "row"), "col")),
        check_vma=False,
    )
```

```python
import functools

import jax
import jax.numpy as jnp
from jax import lax
from jax.experimental import pallas as pl
from jax.experimental.pallas import tpu as pltpu
from jax.sharding import PartitionSpec as P


SLOTS, PIECE = 4, 128


def chip_ring(rows):
    width = 2 if rows <= 8 else 4
    depth = rows // width
    order = [z * width for z in range(depth)]
    for step, z in enumerate(reversed(range(depth))):
        columns = range(1, width) if step % 2 == 0 else range(width - 1, 0, -1)
        order += [z * width + x for x in columns]
    return order


def gram_kernel(scale, left_ref, *refs):
    right_refs, out_ref, turned = refs[:-2], refs[-2], refs[-1]

    @pl.when(pl.program_id(0) == 0)
    def _():
        turned[...] = left_ref[...].T

    right = jnp.concatenate([ref[...] for ref in right_refs], axis=0)
    out_ref[...] = jnp.dot(turned[...], right, preferred_element_type=jnp.float32) * scale


def gram(left, rights, scale, steps, tile):
    tokens, height = left.shape
    return pl.pallas_call(
        functools.partial(gram_kernel, scale),
        grid=(steps,),
        in_specs=[pl.BlockSpec((tokens, height), lambda j: (0, 0))]
        + [pl.BlockSpec((part.shape[0], tile), lambda j: (0, j)) for part in rights],
        out_specs=pl.BlockSpec((height, tile), lambda j: (0, j)),
        out_shape=jax.ShapeDtypeStruct((height, steps * tile), jnp.float32),
        scratch_shapes=[pltpu.VMEM((height, tokens), jnp.bfloat16)],
        compiler_params=pltpu.CompilerParams(vmem_limit_bytes=32 * 1024 * 1024),
    )(left, *rights)


def tiles_kernel(scale, groups, ready, lists, outs, aliased, *refs):
    left_refs, refs = refs[: len(ready)], refs[len(ready) :]
    sources = []
    for shards in lists:
        sources.append(refs[:shards])
        refs = refs[shards:]
    refs = refs[aliased:]
    out_refs, turned = refs[:outs], list(refs[outs:-3])
    joined, buffer, sems = refs[-3:]
    turned = [left_ref if done else turned.pop(0) for left_ref, done in zip(left_refs, ready)]

    def copy(group, slot, j):
        _, height, (_, _, _, width), which, row, column, stride, _ = group
        return pltpu.make_async_copy(
            buffer.at[slot, pl.ds(0, height), pl.ds(0, width)],
            out_refs[which].at[pl.ds(row, height), pl.ds(pl.multiple_of(column + j * stride, 128), width)],
            sems.at[slot],
        )

    earlier, done = None, [index for index, is_ready in enumerate(ready) if is_ready]
    for group in groups:
        left = group[0]
        if left not in done:
            done.append(left)
            turned[left][...] = left_refs[left][...].T

        def step(j, carry, group=group, earlier=earlier):
            left, height, (source, first, apart, width), _, _, _, _, _ = group
            slot = lax.rem(j, SLOTS)
            here = pl.ds(pl.multiple_of(first + j * apart, 128), width)
            joined[:, :width] = jnp.concatenate([ref[:, here] for ref in sources[source]], axis=0)

            @pl.when(j >= SLOTS)
            def _():
                copy(group, slot, 0).wait()

            if earlier is not None:

                @pl.when(j < SLOTS)
                def _():
                    copy(earlier, slot, 0).wait()

            for across in range(0, width, 256):
                right = joined[:, across : across + 256]
                for down in range(0, height, PIECE):
                    rows = turned[left][down : down + PIECE, :]
                    product = jnp.dot(rows, right, preferred_element_type=jnp.float32)
                    buffer[slot, down : down + PIECE, across : across + 256] = product * scale
            copy(group, slot, j).start()
            return carry

        lax.fori_loop(0, group[-1], step, 0)
        earlier = group
    for slot in range(SLOTS):
        copy(earlier, slot, 0).wait()


def tiles(scale, groups, lefts, lists, out_shapes, out=None, ready=(), hand_on=False):
    ready = tuple(ready) or (False,) * len(lefts)
    tokens = lists[0][0].shape[0] * len(lists[0])
    whole, anywhere = pl.BlockSpec(memory_space=pltpu.VMEM), pl.BlockSpec(memory_space=pl.ANY)
    operands = [*lefts, *[part for parts in lists for part in parts]]
    specs, aliases = [whole] * len(operands), {}
    if out is not None:
        aliases = {len(operands): 0}
        operands.append(out)
        specs.append(anywhere)
    area = sum(g[1] * g[2][3] * g[7] for g in groups)
    turned = [(left.shape[1], tokens) for left, done in zip(lefts, ready) if not done]
    results = [jax.ShapeDtypeStruct(shape, jnp.float32) for shape in out_shapes]
    result_specs = [anywhere] * len(results)
    if hand_on:
        results.append(pltpu.VMEM(turned[0], jnp.bfloat16))
        result_specs.append(whole)
    return pl.pallas_call(
        functools.partial(
            tiles_kernel, scale, groups, ready, [len(parts) for parts in lists], len(out_shapes), len(aliases)
        ),
        in_specs=specs,
        out_specs=result_specs,
        out_shape=results,
        scratch_shapes=[pltpu.VMEM(shape, jnp.bfloat16) for shape in turned[int(hand_on) :]]
        + [
            pltpu.VMEM((tokens, max(g[2][3] for g in groups)), jnp.bfloat16),
            pltpu.VMEM((SLOTS, max(g[1] for g in groups), max(g[2][3] for g in groups)), jnp.float32),
            pltpu.SemaphoreType.DMA((SLOTS,)),
        ],
        input_output_aliases=aliases,
        compiler_params=pltpu.CompilerParams(vmem_limit_bytes=32 * 1024 * 1024),
        cost_estimate=pl.CostEstimate(flops=2 * tokens * area, bytes_accessed=4 * area, transcendentals=0),
    )(*operands)


def split_kernel(halves, layouts, half_ref, count_ref, act_ref, grad_ref, *out_refs):
    slots = act_ref.shape[0]
    live = lax.broadcasted_iota(jnp.int32, (slots, 128), 0) < count_ref[0]
    for half in range(halves):
        for flip in (1, 0):

            @pl.when((half_ref[0] + flip) % halves == half)
            def _(half=half, flip=flip):
                for chain, layout in enumerate(layouts):
                    target = 0
                    for source, start, width in layout:
                        ref = (grad_ref, act_ref)[source]
                        first = half * (ref.shape[1] // halves) + start
                        values = ref[:, first : first + width]
                        mask = jnp.concatenate([live] * (width // 128), axis=1)
                        masked = jnp.where(mask, values, jnp.zeros_like(values))
                        own = (half + flip) % halves * slots
                        out_ref, columns = out_refs[2 * chain + flip], slice(target, target + width)
                        out_ref[own : own + slots, columns] = masked
                        other = slots - own
                        out_ref[other : other + slots, columns] = jnp.zeros_like(values)
                        target += width


def solution(mesh):
    rows, cols = mesh.shape["row"], mesh.shape["col"]
    order = chip_ring(rows)
    ahead = [(order[p], order[(p + 1) % rows]) for p in range(rows)]
    behind = [(target, source) for source, target in ahead]
    swap = [(0, 1), (1, 0)]
    half_rows = rows // cols
    scale = 1.0 / (9.0 * rows * cols)

    def local(activations, pseudo_grads, row_counts):
        row, col = lax.axis_index("row"), lax.axis_index("col")
        slots, act_width = activations.shape
        grad_width = pseudo_grads.shape[1]
        act_half, grad_half = act_width // cols, grad_width // cols
        act_block, grad_block = act_width // rows, grad_width // rows
        cut = act_block * 4 // 7 if act_block % 1792 == 0 else act_block
        rest = act_block - cut
        widths = [half_rows * cut, half_rows * rest + grad_half]
        if rest == 0:
            layouts = [[(1, 0, act_half)], [(0, 0, grad_half)]]
        else:
            layouts = [
                [(1, j * act_block, cut) for j in range(half_rows)],
                [(1, j * act_block + cut, rest) for j in range(half_rows)] + [(0, 0, grad_half)],
            ]
        pieces = pl.pallas_call(
            functools.partial(split_kernel, cols, layouts),
            in_specs=[pl.BlockSpec(memory_space=pltpu.SMEM)] * 2 + [pl.BlockSpec(memory_space=pltpu.VMEM)] * 2,
            out_specs=[pl.BlockSpec(memory_space=pltpu.VMEM)] * 4,
            out_shape=[pltpu.VMEM((2 * slots, width), jnp.bfloat16) for width in widths for _ in (0, 1)],
        )(col[None], row_counts, activations, pseudo_grads)
        chains = [[pieces[2 * k] + lax.ppermute(pieces[2 * k + 1], "col", swap)] for k in (0, 1)]
        forward = [chain[0] for chain in chains]
        backward = list(forward)
        steps, halfway = [0] * len(chains), rows // 2
        sequence = [0, 1] * halfway
        def left_part(chain, pieces, hold=None):
            own = []
            for part in chain:
                cuts = [
                    lax.dynamic_slice_in_dim(part, base + (row % half_rows) * size, size, 1) for base, size in pieces
                ]
                own.append(cuts[0] if len(cuts) == 1 else jnp.concatenate(cuts, axis=1))
            groups = [jnp.concatenate(own[:-1], axis=0), own[-1]]
            mine = col == row // half_rows
            if hold is not None:
                hold.append(groups[1])
            return jnp.concatenate([jnp.where(mine, g, lax.ppermute(g, "col", swap)) for g in groups], axis=0)

        previous, hold, left_first = (), [], None
        for k in sequence:
            chain, middle = chains[k], widths[k] // 2
            steps[k] += 1
            final = steps[k] == halfway
            ahead_of, _ = lax.optimization_barrier((forward[k], previous))
            behind_of, _ = lax.optimization_barrier((backward[k], (previous, hold)))
            previous = forward[k]
            if final:
                ahead_of, behind_of = ahead_of[:, :middle], behind_of[:, middle:]
            forward[k] = lax.ppermute(ahead_of, "row", ahead)
            backward[k] = lax.ppermute(behind_of, "row", behind)
            if not final:
                chain += [forward[k], backward[k]]
                latest = (forward[k], backward[k])
            elif k == 0:
                last_first, _ = lax.optimization_barrier(((forward[k], backward[k]), latest))
                chain.append(jnp.concatenate(last_first, axis=1))
                left_first = left_part(chain, [(0, cut)], hold)

        act_shape, grad_shape = (act_block, act_half), (grad_block, grad_half)
        if rest == 0:
            chains[1].append(jnp.concatenate((forward[1], backward[1]), axis=1))
            left_grad = left_part(chains[1], [(0, grad_block)])
            act_cov = gram(left_first, chains[0], scale, act_half // 256, 256)
            grad_cov = gram(left_grad, chains[1], scale, grad_half // 256, 256)
        else:
            grad_first = half_rows * rest
            first_part, second_part = (0, 0, cut, cut), (1, 0, rest, rest)
            grad_part = (1, grad_first, grad_block, grad_block)

            def square(part, lefts, out, **more):
                starts = [part * cut // 2, part * cut // 2 + cut // 4]
                groups = [(0, cut, (0, at, cut, cut // 4), 0, 0, at, act_block, half_rows) for at in starts]
                return tiles(scale, groups, lefts, [chains[0]], [act_shape], out, **more)

            act_cov, turned_first = square(0, [left_first], None, hand_on=True)
            last_second, act_cov = lax.optimization_barrier(((forward[1], backward[1]), act_cov))
            chains[1].append(jnp.concatenate(last_second, axis=1))
            left_second = left_part(chains[1], [(0, rest), (grad_first, grad_block)])
            (act_cov,) = square(1, [turned_first], act_cov, ready=[True])
            act_cov, grad_cov = tiles(
                scale,
                [
                    (2, grad_block, grad_part, 1, 0, 0, grad_block, half_rows),
                    (0, cut, second_part, 0, 0, cut, act_block, half_rows),
                    (1, rest, first_part, 0, cut, 0, act_block, half_rows),
                    (1, rest, second_part, 0, cut, cut, act_block, half_rows),
                ],
                [turned_first, left_second[:, :rest], left_second[:, rest:]],
                chains, [act_shape, grad_shape], act_cov, ready=[True, False, False],
            )
        return act_cov, grad_cov

    return jax.shard_map(
        local,
        mesh=mesh,
        in_specs=(
            P(("groups", "row", "col"), None),
            P(("groups", "row", "col"), None),
            P(("groups", "row", "col")),
        ),
        out_specs=(P(("groups", "row"), "col"), P(("groups", "row"), "col")),
        check_vma=False,
    )
```

```python
import functools

import jax
import jax.numpy as jnp
from jax import lax
from jax.experimental import pallas as pl
from jax.experimental.pallas import tpu as pltpu
from jax.sharding import PartitionSpec as P


SLOTS, PIECE = 4, 128


def chip_ring(rows):
    width = 2 if rows <= 8 else 4
    depth = rows // width
    order = [z * width for z in range(depth)]
    for step, z in enumerate(reversed(range(depth))):
        columns = range(1, width) if step % 2 == 0 else range(width - 1, 0, -1)
        order += [z * width + x for x in columns]
    return order


def gram_kernel(scale, left_ref, *refs):
    right_refs, out_ref, turned = refs[:-2], refs[-2], refs[-1]

    @pl.when(pl.program_id(0) == 0)
    def _():
        turned[...] = left_ref[...].T

    right = jnp.concatenate([ref[...] for ref in right_refs], axis=0)
    out_ref[...] = jnp.dot(turned[...], right, preferred_element_type=jnp.float32) * scale


def gram(left, rights, scale, steps, tile):
    tokens, height = left.shape
    return pl.pallas_call(
        functools.partial(gram_kernel, scale),
        grid=(steps,),
        in_specs=[pl.BlockSpec((tokens, height), lambda j: (0, 0))]
        + [pl.BlockSpec((part.shape[0], tile), lambda j: (0, j)) for part in rights],
        out_specs=pl.BlockSpec((height, tile), lambda j: (0, j)),
        out_shape=jax.ShapeDtypeStruct((height, steps * tile), jnp.float32),
        scratch_shapes=[pltpu.VMEM((height, tokens), jnp.bfloat16)],
        compiler_params=pltpu.CompilerParams(vmem_limit_bytes=32 * 1024 * 1024),
    )(left, *rights)


def tiles_kernel(scale, cut, rest, grad_tile, shards, *refs):
    first_left, second_left = refs[:2]
    first, second = refs[2 : 2 + shards], refs[2 + shards : 2 + 2 * shards]
    act_out, grad_out, turned, turned_grad, joined, buffer, sems = refs[2 + 2 * shards :]
    act_block, blocks = cut + rest, first[0].shape[1] // cut
    groups = [(turned_grad, second, blocks * rest, grad_tile, grad_tile, grad_out, 0, grad_tile, blocks)]
    groups.append((turned, second, 0, rest, rest, act_out, cut, act_block, blocks))
    for start in range(0, cut, 256):
        groups.append((turned, first, start, cut, 256, act_out, start, act_block, blocks))

    def copy(group, slot, j):
        left, _, _, _, width, out, column, stride, _ = group
        return pltpu.make_async_copy(
            buffer.at[slot, pl.ds(0, left.shape[0]), pl.ds(0, width)],
            out.at[:, pl.ds(pl.multiple_of(column + j * stride, 128), width)],
            sems.at[slot],
        )

    turned_grad[...] = second_left[:, rest:].T
    earlier = None
    for group in groups:

        def step(j, carry, group=group, earlier=earlier):
            left, sources, start, apart, width, _, _, _, _ = group
            height, slot = left.shape[0], lax.rem(j, SLOTS)
            here = pl.ds(pl.multiple_of(start + j * apart, 128), width)
            joined[:, :width] = jnp.concatenate([ref[:, here] for ref in sources], axis=0)

            @pl.when(j >= SLOTS)
            def _():
                copy(group, slot, 0).wait()

            if earlier is not None:

                @pl.when(j < SLOTS)
                def _():
                    copy(earlier, slot, 0).wait()

            for across in range(0, width, 256):
                right = joined[:, across : across + 256]
                for down in range(0, height, PIECE):
                    product = jnp.dot(left[down : down + PIECE, :], right, preferred_element_type=jnp.float32)
                    buffer[slot, down : down + PIECE, across : across + 256] = product * scale
            copy(group, slot, j).start()
            return carry

        lax.fori_loop(0, group[-1], step, 0)
        if earlier is None:
            turned[:cut, :] = first_left[...].T
            turned[cut:, :] = second_left[:, :rest].T
        earlier = group
    for slot in range(SLOTS):
        copy(earlier, slot, 0).wait()


def tiles(scale, cut, rest, first_left, second_left, chains):
    shards = len(chains[0])
    tokens, blocks = first_left.shape[0], chains[0][0].shape[1] // cut
    act_block, grad_block = cut + rest, second_left.shape[1] - rest
    grad_half = chains[1][0].shape[1] - blocks * rest
    act_shape, grad_shape = (act_block, blocks * act_block), (grad_block, grad_half)
    area = act_shape[0] * act_shape[1] + grad_shape[0] * grad_shape[1]
    whole = pl.BlockSpec(memory_space=pltpu.VMEM)
    return pl.pallas_call(
        functools.partial(tiles_kernel, scale, cut, rest, grad_half // blocks, shards),
        in_specs=[whole] * (2 + 2 * shards),
        out_specs=[pl.BlockSpec(memory_space=pl.ANY)] * 2,
        out_shape=[jax.ShapeDtypeStruct(shape, jnp.float32) for shape in (act_shape, grad_shape)],
        scratch_shapes=[
            pltpu.VMEM((act_block, tokens), jnp.bfloat16),
            pltpu.VMEM((grad_block, tokens), jnp.bfloat16),
            pltpu.VMEM((tokens, rest), jnp.bfloat16),
            pltpu.VMEM((SLOTS, act_block, rest), jnp.float32),
            pltpu.SemaphoreType.DMA((SLOTS,)),
        ],
        compiler_params=pltpu.CompilerParams(vmem_limit_bytes=40 * 1024 * 1024),
        cost_estimate=pl.CostEstimate(flops=2 * tokens * area, bytes_accessed=4 * area, transcendentals=0),
    )(first_left, second_left, *chains[0], *chains[1])


def split_kernel(halves, layouts, half_ref, count_ref, act_ref, grad_ref, *out_refs):
    slots = act_ref.shape[0]
    live = lax.broadcasted_iota(jnp.int32, (slots, 128), 0) < count_ref[0]
    for half in range(halves):
        for flip in (1, 0):

            @pl.when((half_ref[0] + flip) % halves == half)
            def _(half=half, flip=flip):
                for chain, layout in enumerate(layouts):
                    target = 0
                    for source, start, width in layout:
                        ref = (grad_ref, act_ref)[source]
                        first = half * (ref.shape[1] // halves) + start
                        values = ref[:, first : first + width]
                        mask = jnp.concatenate([live] * (width // 128), axis=1)
                        masked = jnp.where(mask, values, jnp.zeros_like(values))
                        own = (half + flip) % halves * slots
                        out_ref, columns = out_refs[2 * chain + flip], slice(target, target + width)
                        out_ref[own : own + slots, columns] = masked
                        other = slots - own
                        out_ref[other : other + slots, columns] = jnp.zeros_like(values)
                        target += width


def solution(mesh):
    rows, cols = mesh.shape["row"], mesh.shape["col"]
    order = chip_ring(rows)
    ahead = [(order[p], order[(p + 1) % rows]) for p in range(rows)]
    behind = [(target, source) for source, target in ahead]
    swap = [(0, 1), (1, 0)]
    half_rows = rows // cols
    scale = 1.0 / (9.0 * rows * cols)

    def local(activations, pseudo_grads, row_counts):
        row, col = lax.axis_index("row"), lax.axis_index("col")
        slots, act_width = activations.shape
        grad_width = pseudo_grads.shape[1]
        act_half, grad_half = act_width // cols, grad_width // cols
        act_block, grad_block = act_width // rows, grad_width // rows
        cut = act_block * 4 // 7 if act_block % 1792 == 0 else act_block
        rest = act_block - cut
        widths = [half_rows * cut, half_rows * rest + grad_half]
        if rest == 0:
            layouts = [[(1, 0, act_half)], [(0, 0, grad_half)]]
        else:
            layouts = [
                [(1, j * act_block, cut) for j in range(half_rows)],
                [(1, j * act_block + cut, rest) for j in range(half_rows)] + [(0, 0, grad_half)],
            ]
        pieces = pl.pallas_call(
            functools.partial(split_kernel, cols, layouts),
            in_specs=[pl.BlockSpec(memory_space=pltpu.SMEM)] * 2 + [pl.BlockSpec(memory_space=pltpu.VMEM)] * 2,
            out_specs=[pl.BlockSpec(memory_space=pltpu.VMEM)] * 4,
            out_shape=[pltpu.VMEM((2 * slots, width), jnp.bfloat16) for width in widths for _ in (0, 1)],
        )(col[None], row_counts, activations, pseudo_grads)
        chains = [[pieces[2 * k] + lax.ppermute(pieces[2 * k + 1], "col", swap)] for k in (0, 1)]
        forward = [chain[0] for chain in chains]
        backward = list(forward)
        steps, halfway = [0] * len(chains), rows // 2
        sequence = [0, 1] * halfway
        def left_part(chain, pieces):
            own = []
            for part in chain:
                cuts = [
                    lax.dynamic_slice_in_dim(part, base + (row % half_rows) * size, size, 1) for base, size in pieces
                ]
                own.append(cuts[0] if len(cuts) == 1 else jnp.concatenate(cuts, axis=1))
            groups = [jnp.concatenate(own[:-1], axis=0), own[-1]]
            mine = col == row // half_rows
            return jnp.concatenate([jnp.where(mine, g, lax.ppermute(g, "col", swap)) for g in groups], axis=0)

        previous = ()
        for k in sequence:
            chain = chains[k]
            steps[k] += 1
            ahead_of, _ = lax.optimization_barrier((forward[k], previous))
            behind_of, _ = lax.optimization_barrier((backward[k], previous))
            previous = forward[k]
            if steps[k] < halfway or k == 0:
                forward[k] = lax.ppermute(ahead_of, "row", ahead)
                chain.append(forward[k])
            if steps[k] < halfway or k == 1:
                backward[k] = lax.ppermute(behind_of, "row", behind)
                chain.append(backward[k])

        left_first = left_part(chains[0], [(0, cut)])
        if rest == 0:
            left_grad = left_part(chains[1], [(0, grad_block)])
            act_cov = gram(left_first, chains[0], scale, act_half // 256, 256)
            grad_cov = gram(left_grad, chains[1], scale, grad_half // 256, 256)
        else:
            left_second = left_part(chains[1], [(0, rest), (half_rows * rest, grad_block)])
            act_cov, grad_cov = tiles(scale, cut, rest, left_first, left_second, chains)
        return act_cov, grad_cov

    return jax.shard_map(
        local,
        mesh=mesh,
        in_specs=(
            P(("groups", "row", "col"), None),
            P(("groups", "row", "col"), None),
            P(("groups", "row", "col")),
        ),
        out_specs=(P(("groups", "row"), "col"), P(("groups", "row"), "col")),
        check_vma=False,
    )
```

```python
import functools

import jax
import jax.numpy as jnp
from jax import lax
from jax.experimental import pallas as pl
from jax.experimental.pallas import tpu as pltpu
from jax.sharding import PartitionSpec as P


SLOTS, PIECE = 4, 128


def chip_ring(rows):
    width = 2 if rows <= 8 else 4
    depth = rows // width
    order = [z * width for z in range(depth)]
    for step, z in enumerate(reversed(range(depth))):
        columns = range(1, width) if step % 2 == 0 else range(width - 1, 0, -1)
        order += [z * width + x for x in columns]
    return order


def gram_kernel(scale, left_ref, *refs):
    right_refs, out_ref, turned = refs[:-2], refs[-2], refs[-1]

    @pl.when(pl.program_id(0) == 0)
    def _():
        turned[...] = left_ref[...].T

    right = jnp.concatenate([ref[...] for ref in right_refs], axis=0)
    out_ref[...] = jnp.dot(turned[...], right, preferred_element_type=jnp.float32) * scale


def gram(left, rights, scale, steps, tile):
    tokens, height = left.shape
    return pl.pallas_call(
        functools.partial(gram_kernel, scale),
        grid=(steps,),
        in_specs=[pl.BlockSpec((tokens, height), lambda j: (0, 0))]
        + [pl.BlockSpec((part.shape[0], tile), lambda j: (0, j)) for part in rights],
        out_specs=pl.BlockSpec((height, tile), lambda j: (0, j)),
        out_shape=jax.ShapeDtypeStruct((height, steps * tile), jnp.float32),
        scratch_shapes=[pltpu.VMEM((height, tokens), jnp.bfloat16)],
        compiler_params=pltpu.CompilerParams(vmem_limit_bytes=32 * 1024 * 1024),
    )(left, *rights)


def tiles_kernel(scale, groups, ready, lists, outs, aliased, *refs):
    left_refs, refs = refs[: len(ready)], refs[len(ready) :]
    sources = []
    for shards in lists:
        sources.append(refs[:shards])
        refs = refs[shards:]
    refs = refs[aliased:]
    out_refs, turned = refs[:outs], list(refs[outs:-3])
    joined, buffer, sems = refs[-3:]
    turned = [left_ref if done else turned.pop(0) for left_ref, done in zip(left_refs, ready)]

    def copy(group, slot, j):
        _, height, (_, _, _, width), which, row, column, stride, _ = group
        return pltpu.make_async_copy(
            buffer.at[slot, pl.ds(0, height), pl.ds(0, width)],
            out_refs[which].at[pl.ds(row, height), pl.ds(pl.multiple_of(column + j * stride, 128), width)],
            sems.at[slot],
        )

    earlier, done = None, [index for index, is_ready in enumerate(ready) if is_ready]
    for group in groups:
        left = group[0]
        if left not in done:
            done.append(left)
            turned[left][...] = left_refs[left][...].T

        def step(j, carry, group=group, earlier=earlier):
            left, height, (source, first, apart, width), _, _, _, _, _ = group
            slot = lax.rem(j, SLOTS)
            here = pl.ds(pl.multiple_of(first + j * apart, 128), width)
            joined[:, :width] = jnp.concatenate([ref[:, here] for ref in sources[source]], axis=0)

            @pl.when(j >= SLOTS)
            def _():
                copy(group, slot, 0).wait()

            if earlier is not None:

                @pl.when(j < SLOTS)
                def _():
                    copy(earlier, slot, 0).wait()

            for across in range(0, width, 256):
                right = joined[:, across : across + 256]
                for down in range(0, height, PIECE):
                    rows = turned[left][down : down + PIECE, :]
                    product = jnp.dot(rows, right, preferred_element_type=jnp.float32)
                    buffer[slot, down : down + PIECE, across : across + 256] = product * scale
            copy(group, slot, j).start()
            return carry

        lax.fori_loop(0, group[-1], step, 0)
        earlier = group
    for slot in range(SLOTS):
        copy(earlier, slot, 0).wait()


def tiles(scale, groups, lefts, lists, out_shapes, out=None, ready=(), hand_on=False):
    ready = tuple(ready) or (False,) * len(lefts)
    tokens = lists[0][0].shape[0] * len(lists[0])
    whole, anywhere = pl.BlockSpec(memory_space=pltpu.VMEM), pl.BlockSpec(memory_space=pl.ANY)
    operands = [*lefts, *[part for parts in lists for part in parts]]
    specs, aliases = [whole] * len(operands), {}
    if out is not None:
        aliases = {len(operands): 0}
        operands.append(out)
        specs.append(anywhere)
    area = sum(g[1] * g[2][3] * g[7] for g in groups)
    turned = [(left.shape[1], tokens) for left, done in zip(lefts, ready) if not done]
    results = [jax.ShapeDtypeStruct(shape, jnp.float32) for shape in out_shapes]
    result_specs = [anywhere] * len(results)
    if hand_on:
        results.append(pltpu.VMEM(turned[0], jnp.bfloat16))
        result_specs.append(whole)
    return pl.pallas_call(
        functools.partial(
            tiles_kernel, scale, groups, ready, [len(parts) for parts in lists], len(out_shapes), len(aliases)
        ),
        in_specs=specs,
        out_specs=result_specs,
        out_shape=results,
        scratch_shapes=[pltpu.VMEM(shape, jnp.bfloat16) for shape in turned[int(hand_on) :]]
        + [
            pltpu.VMEM((tokens, max(g[2][3] for g in groups)), jnp.bfloat16),
            pltpu.VMEM((SLOTS, max(g[1] for g in groups), max(g[2][3] for g in groups)), jnp.float32),
            pltpu.SemaphoreType.DMA((SLOTS,)),
        ],
        input_output_aliases=aliases,
        compiler_params=pltpu.CompilerParams(vmem_limit_bytes=32 * 1024 * 1024),
        cost_estimate=pl.CostEstimate(flops=2 * tokens * area, bytes_accessed=4 * area, transcendentals=0),
    )(*operands)


def split_kernel(halves, layouts, half_ref, count_ref, act_ref, grad_ref, *out_refs):
    slots = act_ref.shape[0]
    live = lax.broadcasted_iota(jnp.int32, (slots, 128), 0) < count_ref[0]
    for half in range(halves):
        for flip in (1, 0):

            @pl.when((half_ref[0] + flip) % halves == half)
            def _(half=half, flip=flip):
                for chain, layout in enumerate(layouts):
                    target = 0
                    for source, start, width in layout:
                        ref = (grad_ref, act_ref)[source]
                        first = half * (ref.shape[1] // halves) + start
                        values = ref[:, first : first + width]
                        mask = jnp.concatenate([live] * (width // 128), axis=1)
                        masked = jnp.where(mask, values, jnp.zeros_like(values))
                        own = (half + flip) % halves * slots
                        out_ref, columns = out_refs[2 * chain + flip], slice(target, target + width)
                        out_ref[own : own + slots, columns] = masked
                        other = slots - own
                        out_ref[other : other + slots, columns] = jnp.zeros_like(values)
                        target += width


def solution(mesh):
    rows, cols = mesh.shape["row"], mesh.shape["col"]
    order = chip_ring(rows)
    ahead = [(order[p], order[(p + 1) % rows]) for p in range(rows)]
    behind = [(target, source) for source, target in ahead]
    swap = [(0, 1), (1, 0)]
    half_rows = rows // cols
    across = [
        (source * cols + target // half_rows, target * cols + 1 - target // half_rows) for source, target in behind
    ]
    scale = 1.0 / (9.0 * rows * cols)

    def local(activations, pseudo_grads, row_counts):
        row, col = lax.axis_index("row"), lax.axis_index("col")
        slots, act_width = activations.shape
        grad_width = pseudo_grads.shape[1]
        act_half, grad_half = act_width // cols, grad_width // cols
        act_block, grad_block = act_width // rows, grad_width // rows
        cut = act_block * 4 // 7 if act_block % 1792 == 0 else act_block
        rest = act_block - cut
        widths = [half_rows * cut, half_rows * rest + grad_half]
        if rest == 0:
            layouts = [[(1, 0, act_half)], [(0, 0, grad_half)]]
        else:
            layouts = [
                [(1, j * act_block, cut) for j in range(half_rows)],
                [(1, j * act_block + cut, rest) for j in range(half_rows)] + [(0, 0, grad_half)],
            ]
        pieces = pl.pallas_call(
            functools.partial(split_kernel, cols, layouts),
            in_specs=[pl.BlockSpec(memory_space=pltpu.SMEM)] * 2 + [pl.BlockSpec(memory_space=pltpu.VMEM)] * 2,
            out_specs=[pl.BlockSpec(memory_space=pltpu.VMEM)] * 4,
            out_shape=[pltpu.VMEM((2 * slots, width), jnp.bfloat16) for width in widths for _ in (0, 1)],
        )(col[None], row_counts, activations, pseudo_grads)
        chains = [[pieces[2 * k] + lax.ppermute(pieces[2 * k + 1], "col", swap)] for k in (0, 1)]
        forward = [chain[0] for chain in chains]
        backward = list(forward)
        steps, halfway = [0] * len(chains), rows // 2
        sequence = [0, 1] * halfway
        mine = col == row // half_rows

        def block_of(part, pieces, block_row):
            cuts = [
                lax.dynamic_slice_in_dim(part, base + (block_row % half_rows) * size, size, 1) for base, size in pieces
            ]
            return cuts[0] if len(cuts) == 1 else jnp.concatenate(cuts, axis=1)

        def left_part(chain, pieces, direct=None):
            own = [block_of(part, pieces, row) for part in chain]
            early = jnp.concatenate(own[:-1], axis=0)
            late = lax.ppermute(own[-1], "col", swap) if direct is None else direct
            early = jnp.where(mine, early, lax.ppermute(early, "col", swap))
            return jnp.concatenate([early, jnp.where(mine, own[-1], late)], axis=0)

        first_pieces = [(0, cut)]
        second_pieces = [(0, rest), (half_rows * rest, grad_block)] if rest else [(0, grad_block)]
        previous = ()
        for k in sequence:
            chain = chains[k]
            steps[k] += 1
            ahead_of, _ = lax.optimization_barrier((forward[k], previous))
            behind_of, _ = lax.optimization_barrier((backward[k], previous))
            previous = forward[k]
            if steps[k] < halfway or k == 0:
                forward[k] = lax.ppermute(ahead_of, "row", ahead)
                chain.append(forward[k])
            if steps[k] < halfway or k == 1:
                backward[k] = lax.ppermute(behind_of, "row", behind)
                chain.append(backward[k])
            if steps[k] == halfway and k == 1:
                receiver = jnp.asarray([target for _, target in sorted(behind)], jnp.int32)[row]
                direct = lax.ppermute(block_of(behind_of, second_pieces, receiver), ("row", "col"), across)

        left_first = left_part(chains[0], first_pieces)
        if rest == 0:
            left_grad = left_part(chains[1], second_pieces, direct)
            act_cov = gram(left_first, chains[0], scale, act_half // 256, 256)
            grad_cov = gram(left_grad, chains[1], scale, grad_half // 256, 256)
        else:
            first_part, second_part = (0, 0, cut, cut), (1, 0, rest, rest)
            grad_part = (1, half_rows * rest, grad_block, grad_block)
            act_shape, grad_shape = (act_block, act_half), (grad_block, grad_half)
            groups = [
                (0, cut, (0, start, cut, cut // 2), 0, 0, start, act_block, half_rows) for start in (0, cut // 2)
            ]
            act_cov, turned_first = tiles(scale, groups, [left_first], [chains[0]], [act_shape], hand_on=True)
            (chains[1][-1], direct), act_cov = lax.optimization_barrier(((chains[1][-1], direct), act_cov))
            left_second = left_part(chains[1], second_pieces, direct)
            act_cov, grad_cov = tiles(
                scale,
                [
                    (2, grad_block, grad_part, 1, 0, 0, grad_block, half_rows),
                    (0, cut, second_part, 0, 0, cut, act_block, half_rows),
                    (1, rest, first_part, 0, cut, 0, act_block, half_rows),
                    (1, rest, second_part, 0, cut, cut, act_block, half_rows),
                ],
                [turned_first, left_second[:, :rest], left_second[:, rest:]],
                chains, [act_shape, grad_shape], act_cov, ready=[True, False, False],
            )
        return act_cov, grad_cov

    return jax.shard_map(
        local,
        mesh=mesh,
        in_specs=(
            P(("groups", "row", "col"), None),
            P(("groups", "row", "col"), None),
            P(("groups", "row", "col")),
        ),
        out_specs=(P(("groups", "row"), "col"), P(("groups", "row"), "col")),
        check_vma=False,
    )
```

```python
import functools

import jax
import jax.numpy as jnp
from jax import lax
from jax.experimental import pallas as pl
from jax.experimental.pallas import tpu as pltpu
from jax.sharding import PartitionSpec as P


SLOTS, PIECE = 4, 128


def chip_ring(rows):
    width = 2 if rows <= 8 else 4
    depth = rows // width
    order = [z * width for z in range(depth)]
    for step, z in enumerate(reversed(range(depth))):
        columns = range(1, width) if step % 2 == 0 else range(width - 1, 0, -1)
        order += [z * width + x for x in columns]
    return order


def gram_kernel(scale, left_ref, *refs):
    right_refs, out_ref, turned = refs[:-2], refs[-2], refs[-1]

    @pl.when(pl.program_id(0) == 0)
    def _():
        turned[...] = left_ref[...].T

    right = jnp.concatenate([ref[...] for ref in right_refs], axis=0)
    out_ref[...] = jnp.dot(turned[...], right, preferred_element_type=jnp.float32) * scale


def gram(left, rights, scale, steps, tile):
    tokens, height = left.shape
    return pl.pallas_call(
        functools.partial(gram_kernel, scale),
        grid=(steps,),
        in_specs=[pl.BlockSpec((tokens, height), lambda j: (0, 0))]
        + [pl.BlockSpec((part.shape[0], tile), lambda j: (0, j)) for part in rights],
        out_specs=pl.BlockSpec((height, tile), lambda j: (0, j)),
        out_shape=jax.ShapeDtypeStruct((height, steps * tile), jnp.float32),
        scratch_shapes=[pltpu.VMEM((height, tokens), jnp.bfloat16)],
        compiler_params=pltpu.CompilerParams(vmem_limit_bytes=32 * 1024 * 1024),
    )(left, *rights)


def tiles_kernel(scale, groups, ready, lists, outs, aliased, *refs):
    left_refs, refs = refs[: len(ready)], refs[len(ready) :]
    sources = []
    for shards in lists:
        sources.append(refs[:shards])
        refs = refs[shards:]
    refs = refs[aliased:]
    out_refs, turned = refs[:outs], list(refs[outs:-3])
    joined, buffer, sems = refs[-3:]
    turned = [left_ref if done else turned.pop(0) for left_ref, done in zip(left_refs, ready)]

    def copy(group, slot, j, part=0, parts=1):
        _, height, (_, _, _, width), which, row, column, stride, _ = group
        rows = height // parts
        return pltpu.make_async_copy(
            buffer.at[slot, pl.ds(part * rows, rows), pl.ds(0, width)],
            out_refs[which].at[
                pl.ds(row + part * rows, rows), pl.ds(pl.multiple_of(column + j * stride, 128), width)
            ],
            sems.at[slot],
        )

    earlier, done = None, [index for index, is_ready in enumerate(ready) if is_ready]
    for group in groups:
        left = group[0]
        if left not in done:
            done.append(left)
            turned[left][...] = left_refs[left][...].T

        def step(j, carry, group=group, earlier=earlier):
            left, height, (source, first, apart, width), _, _, _, _, _ = group
            slot = lax.rem(j, SLOTS)
            here = pl.ds(pl.multiple_of(first + j * apart, 128), width)
            joined[:, :width] = jnp.concatenate([ref[:, here] for ref in sources[source]], axis=0)

            @pl.when(j >= SLOTS)
            def _():
                copy(group, slot, 0).wait()

            if earlier is not None:

                @pl.when(j < SLOTS)
                def _():
                    copy(earlier, slot, 0).wait()

            for across in range(0, width, 256):
                right = joined[:, across : across + 256]
                for down in range(0, height, PIECE):
                    rows = turned[left][down : down + PIECE, :]
                    product = jnp.dot(rows, right, preferred_element_type=jnp.float32)
                    buffer[slot, down : down + PIECE, across : across + 256] = product * scale
            for part in (0, 1):
                copy(group, slot, j, part, 2).start(priority=part)
            return carry

        lax.fori_loop(0, group[-1], step, 0)
        earlier = group
    for slot in range(SLOTS):
        copy(earlier, slot, 0).wait()


def tiles(scale, groups, lefts, lists, out_shapes, out=None, ready=(), hand_on=False):
    ready = tuple(ready) or (False,) * len(lefts)
    tokens = lists[0][0].shape[0] * len(lists[0])
    whole, anywhere = pl.BlockSpec(memory_space=pltpu.VMEM), pl.BlockSpec(memory_space=pl.ANY)
    operands = [*lefts, *[part for parts in lists for part in parts]]
    specs, aliases = [whole] * len(operands), {}
    if out is not None:
        aliases = {len(operands): 0}
        operands.append(out)
        specs.append(anywhere)
    area = sum(g[1] * g[2][3] * g[7] for g in groups)
    turned = [(left.shape[1], tokens) for left, done in zip(lefts, ready) if not done]
    results = [jax.ShapeDtypeStruct(shape, jnp.float32) for shape in out_shapes]
    result_specs = [anywhere] * len(results)
    if hand_on:
        results.append(pltpu.VMEM(turned[0], jnp.bfloat16))
        result_specs.append(whole)
    return pl.pallas_call(
        functools.partial(
            tiles_kernel, scale, groups, ready, [len(parts) for parts in lists], len(out_shapes), len(aliases)
        ),
        in_specs=specs,
        out_specs=result_specs,
        out_shape=results,
        scratch_shapes=[pltpu.VMEM(shape, jnp.bfloat16) for shape in turned[int(hand_on) :]]
        + [
            pltpu.VMEM((tokens, max(g[2][3] for g in groups)), jnp.bfloat16),
            pltpu.VMEM((SLOTS, max(g[1] for g in groups), max(g[2][3] for g in groups)), jnp.float32),
            pltpu.SemaphoreType.DMA((SLOTS,)),
        ],
        input_output_aliases=aliases,
        compiler_params=pltpu.CompilerParams(vmem_limit_bytes=32 * 1024 * 1024),
        cost_estimate=pl.CostEstimate(flops=2 * tokens * area, bytes_accessed=4 * area, transcendentals=0),
    )(*operands)


def split_kernel(halves, layouts, half_ref, count_ref, act_ref, grad_ref, *out_refs):
    slots = act_ref.shape[0]
    live = lax.broadcasted_iota(jnp.int32, (slots, 128), 0) < count_ref[0]
    for half in range(halves):
        for flip in (1, 0):

            @pl.when((half_ref[0] + flip) % halves == half)
            def _(half=half, flip=flip):
                for chain, layout in enumerate(layouts):
                    target = 0
                    for source, start, width in layout:
                        ref = (grad_ref, act_ref)[source]
                        first = half * (ref.shape[1] // halves) + start
                        values = ref[:, first : first + width]
                        mask = jnp.concatenate([live] * (width // 128), axis=1)
                        masked = jnp.where(mask, values, jnp.zeros_like(values))
                        own = (half + flip) % halves * slots
                        out_ref, columns = out_refs[2 * chain + flip], slice(target, target + width)
                        out_ref[own : own + slots, columns] = masked
                        other = slots - own
                        out_ref[other : other + slots, columns] = jnp.zeros_like(values)
                        target += width


def solution(mesh):
    rows, cols = mesh.shape["row"], mesh.shape["col"]
    order = chip_ring(rows)
    ahead = [(order[p], order[(p + 1) % rows]) for p in range(rows)]
    behind = [(target, source) for source, target in ahead]
    swap = [(0, 1), (1, 0)]
    half_rows = rows // cols
    across = [
        (source * cols + target // half_rows, target * cols + 1 - target // half_rows) for source, target in behind
    ]
    scale = 1.0 / (9.0 * rows * cols)

    def local(activations, pseudo_grads, row_counts):
        row, col = lax.axis_index("row"), lax.axis_index("col")
        slots, act_width = activations.shape
        grad_width = pseudo_grads.shape[1]
        act_half, grad_half = act_width // cols, grad_width // cols
        act_block, grad_block = act_width // rows, grad_width // rows
        cut = act_block * 4 // 7 if act_block % 1792 == 0 else act_block
        rest = act_block - cut
        widths = [half_rows * cut, half_rows * rest + grad_half]
        if rest == 0:
            layouts = [[(1, 0, act_half)], [(0, 0, grad_half)]]
        else:
            layouts = [
                [(1, j * act_block, cut) for j in range(half_rows)],
                [(1, j * act_block + cut, rest) for j in range(half_rows)] + [(0, 0, grad_half)],
            ]
        pieces = pl.pallas_call(
            functools.partial(split_kernel, cols, layouts),
            in_specs=[pl.BlockSpec(memory_space=pltpu.SMEM)] * 2 + [pl.BlockSpec(memory_space=pltpu.VMEM)] * 2,
            out_specs=[pl.BlockSpec(memory_space=pltpu.VMEM)] * 4,
            out_shape=[pltpu.VMEM((2 * slots, width), jnp.bfloat16) for width in widths for _ in (0, 1)],
        )(col[None], row_counts, activations, pseudo_grads)
        chains = [[pieces[2 * k] + lax.ppermute(pieces[2 * k + 1], "col", swap)] for k in (0, 1)]
        forward = [chain[0] for chain in chains]
        backward = list(forward)
        steps, halfway = [0] * len(chains), rows // 2
        sequence = [0, 1] * halfway
        mine = col == row // half_rows

        def block_of(part, pieces, block_row):
            cuts = [
                lax.dynamic_slice_in_dim(part, base + (block_row % half_rows) * size, size, 1) for base, size in pieces
            ]
            return cuts[0] if len(cuts) == 1 else jnp.concatenate(cuts, axis=1)

        def early_part(chain, pieces):
            early = jnp.concatenate([block_of(part, pieces, row) for part in chain[:-1]], axis=0)
            return early, lax.ppermute(early, "col", swap)

        def left_part(early, part, pieces, late):
            own = block_of(part, pieces, row)
            if late is None:
                own, early = lax.optimization_barrier((own, early))
                late = lax.ppermute(own, "col", swap)
            return jnp.concatenate([jnp.where(mine, *early), jnp.where(mine, own, late)], axis=0)

        first_pieces = [(0, cut)]
        second_pieces = [(0, rest), (half_rows * rest, grad_block)] if rest else [(0, grad_block)]
        previous = ()
        for k in sequence:
            chain = chains[k]
            steps[k] += 1
            ahead_of, _ = lax.optimization_barrier((forward[k], previous))
            behind_of, _ = lax.optimization_barrier((backward[k], previous))
            previous = forward[k]
            if steps[k] < halfway or k == 0:
                forward[k] = lax.ppermute(ahead_of, "row", ahead)
                chain.append(forward[k])
            if steps[k] < halfway or k == 1:
                backward[k] = lax.ppermute(behind_of, "row", behind)
                chain.append(backward[k])
            if steps[k] == halfway and k == 1:
                receiver = sum(jnp.where(row == source, target, 0) for source, target in behind)
                direct = lax.ppermute(block_of(behind_of, second_pieces, receiver), ("row", "col"), across)

        early_first, early_second = early_part(chains[0], first_pieces), early_part(chains[1], second_pieces)
        early_first, early_second = lax.optimization_barrier((early_first, early_second))
        left_first = left_part(early_first, chains[0][-1], first_pieces, None)
        if rest == 0:
            left_grad = left_part(early_second, chains[1][-1], second_pieces, direct)
            act_cov = gram(left_first, chains[0], scale, act_half // 256, 256)
            grad_cov = gram(left_grad, chains[1], scale, grad_half // 256, 256)
        else:
            first_part, second_part = (0, 0, cut, cut), (1, 0, rest, rest)
            grad_part = (1, half_rows * rest, grad_block, grad_block)
            act_shape, grad_shape = (act_block, act_half), (grad_block, grad_half)
            groups = [
                (0, cut, (0, start, cut, cut // 2), 0, 0, start, act_block, half_rows) for start in (0, cut // 2)
            ]
            act_cov, turned_first = tiles(scale, groups, [left_first], [chains[0]], [act_shape], hand_on=True)
            (chains[1][-1], direct), act_cov = lax.optimization_barrier(((chains[1][-1], direct), act_cov))
            left_second = left_part(early_second, chains[1][-1], second_pieces, direct)
            act_cov, grad_cov = tiles(
                scale,
                [
                    (2, grad_block, grad_part, 1, 0, 0, grad_block, half_rows),
                    (0, cut, second_part, 0, 0, cut, act_block, half_rows),
                    (1, rest, first_part, 0, cut, 0, act_block, half_rows),
                    (1, rest, second_part, 0, cut, cut, act_block, half_rows),
                ],
                [turned_first, left_second[:, :rest], left_second[:, rest:]],
                chains, [act_shape, grad_shape], act_cov, ready=[True, False, False],
            )
        return act_cov, grad_cov

    return jax.shard_map(
        local,
        mesh=mesh,
        in_specs=(
            P(("groups", "row", "col"), None),
            P(("groups", "row", "col"), None),
            P(("groups", "row", "col")),
        ),
        out_specs=(P(("groups", "row"), "col"), P(("groups", "row"), "col")),
        check_vma=False,
    )
```

```python
import functools

import jax
import jax.numpy as jnp
from jax import lax
from jax.experimental import pallas as pl
from jax.experimental.pallas import tpu as pltpu
from jax.sharding import PartitionSpec as P


SLOTS, PIECE = 4, 128


def chip_ring(rows):
    width = 2 if rows <= 8 else 4
    depth = rows // width
    order = [z * width for z in range(depth)]
    for step, z in enumerate(reversed(range(depth))):
        columns = range(1, width) if step % 2 == 0 else range(width - 1, 0, -1)
        order += [z * width + x for x in columns]
    return order


def gram_kernel(scale, left_ref, *refs):
    right_refs, out_ref, turned = refs[:-2], refs[-2], refs[-1]

    @pl.when(pl.program_id(0) == 0)
    def _():
        turned[...] = left_ref[...].T

    right = jnp.concatenate([ref[...] for ref in right_refs], axis=0)
    out_ref[...] = jnp.dot(turned[...], right, preferred_element_type=jnp.float32) * scale


def gram(left, rights, scale, steps, tile):
    tokens, height = left.shape
    return pl.pallas_call(
        functools.partial(gram_kernel, scale),
        grid=(steps,),
        in_specs=[pl.BlockSpec((tokens, height), lambda j: (0, 0))]
        + [pl.BlockSpec((part.shape[0], tile), lambda j: (0, j)) for part in rights],
        out_specs=pl.BlockSpec((height, tile), lambda j: (0, j)),
        out_shape=jax.ShapeDtypeStruct((height, steps * tile), jnp.float32),
        scratch_shapes=[pltpu.VMEM((height, tokens), jnp.bfloat16)],
        compiler_params=pltpu.CompilerParams(vmem_limit_bytes=32 * 1024 * 1024),
    )(left, *rights)


def tiles_kernel(scale, groups, ready, lists, outs, aliased, *refs):
    left_refs, refs = refs[: len(ready)], refs[len(ready) :]
    sources = []
    for shards in lists:
        sources.append(refs[:shards])
        refs = refs[shards:]
    refs = refs[aliased:]
    out_refs, turned = refs[:outs], list(refs[outs:-3])
    joined, buffer, sems = refs[-3:]
    turned = [left_ref if done else turned.pop(0) for left_ref, done in zip(left_refs, ready)]

    def shape_of(group):
        return group[1] // group[2], sum(part[3] for part in group[3])

    def copy(group, slot, j, m):
        (height, width), (which, row, column, stride) = shape_of(group), group[4:8]
        return pltpu.make_async_copy(
            buffer.at[slot, pl.ds(0, height), pl.ds(0, width)],
            out_refs[which].at[
                pl.ds(pl.multiple_of(row + m * height, 8), height),
                pl.ds(pl.multiple_of(column + j * stride, 128), width),
            ],
            sems.at[slot],
        )

    earlier, done = None, [index for index, is_ready in enumerate(ready) if is_ready]
    for group in groups:
        left = group[0]
        if left not in done:
            done.append(left)
            turned[left][...] = left_refs[left][...].T

        def step(n, carry, group=group, earlier=earlier):
            (height, width), pieces = shape_of(group), group[2]
            slot, j, m = lax.rem(n, SLOTS), lax.div(n, pieces), lax.rem(n, pieces)

            @pl.when(m == 0)
            def _():
                at = 0
                for source, first, apart, wide in group[3]:
                    here = pl.ds(pl.multiple_of(first + j * apart, 128), wide)
                    joined[:, at : at + wide] = jnp.concatenate([ref[:, here] for ref in sources[source]], axis=0)
                    at += wide

            @pl.when(n >= SLOTS)
            def _():
                copy(group, slot, 0, 0).wait()

            if earlier is not None:

                @pl.when(n < SLOTS)
                def _():
                    copy(earlier, slot, 0, 0).wait()

            for across in range(0, width, 256):
                right = joined[:, across : across + 256]
                for down in range(0, height, PIECE):
                    rows = turned[group[0]][pl.ds(pl.multiple_of(m * height + down, 128), PIECE), :]
                    product = jnp.dot(rows, right, preferred_element_type=jnp.float32)
                    buffer[slot, down : down + PIECE, across : across + 256] = product * scale
            copy(group, slot, j, m).start()
            return carry

        lax.fori_loop(0, group[2] * group[-1], step, 0)
        earlier = group
    for slot in range(SLOTS):
        copy(earlier, slot, 0, 0).wait()


def tiles(scale, groups, lefts, lists, out_shapes, out=None, ready=(), hand_on=False):
    ready = tuple(ready) or (False,) * len(lefts)
    tokens = lists[0][0].shape[0] * len(lists[0])
    whole, anywhere = pl.BlockSpec(memory_space=pltpu.VMEM), pl.BlockSpec(memory_space=pl.ANY)
    operands = [*lefts, *[part for parts in lists for part in parts]]
    specs, aliases = [whole] * len(operands), {}
    if out is not None:
        aliases = {len(operands): 0}
        operands.append(out)
        specs.append(anywhere)
    widths = [sum(part[3] for part in g[3]) for g in groups]
    area = sum(g[1] * width * g[8] for g, width in zip(groups, widths))
    turned = [(left.shape[1], tokens) for left, done in zip(lefts, ready) if not done]
    results = [jax.ShapeDtypeStruct(shape, jnp.float32) for shape in out_shapes]
    result_specs = [anywhere] * len(results)
    if hand_on:
        results.append(pltpu.VMEM(turned[0], jnp.bfloat16))
        result_specs.append(whole)
    return pl.pallas_call(
        functools.partial(
            tiles_kernel, scale, groups, ready, [len(parts) for parts in lists], len(out_shapes), len(aliases)
        ),
        in_specs=specs,
        out_specs=result_specs,
        out_shape=results,
        scratch_shapes=[pltpu.VMEM(shape, jnp.bfloat16) for shape in turned[int(hand_on) :]]
        + [
            pltpu.VMEM((tokens, max(widths)), jnp.bfloat16),
            pltpu.VMEM((SLOTS, max(g[1] // g[2] for g in groups), max(widths)), jnp.float32),
            pltpu.SemaphoreType.DMA((SLOTS,)),
        ],
        input_output_aliases=aliases,
        compiler_params=pltpu.CompilerParams(vmem_limit_bytes=32 * 1024 * 1024),
        cost_estimate=pl.CostEstimate(flops=2 * tokens * area, bytes_accessed=4 * area, transcendentals=0),
    )(*operands)


def split_kernel(halves, layout, half_ref, count_ref, *refs):
    sources, out_refs = refs[:-2], refs[-2:]
    slots = sources[0].shape[0]
    live = lax.broadcasted_iota(jnp.int32, (slots, 128), 0) < count_ref[0]
    for half in range(halves):
        for flip in (1, 0):

            @pl.when((half_ref[0] + flip) % halves == half)
            def _(half=half, flip=flip):
                own, target = (half + flip) % halves * slots, 0
                for source, start, width in layout:
                    first = half * (sources[source].shape[1] // halves) + start
                    values = sources[source][:, first : first + width]
                    mask = jnp.concatenate([live] * (width // 128), axis=1)
                    columns = slice(target, target + width)
                    out_refs[flip][own : own + slots, columns] = jnp.where(mask, values, jnp.zeros_like(values))
                    out_refs[flip][slots - own : 2 * slots - own, columns] = jnp.zeros_like(values)
                    target += width


def solution(mesh):
    rows, cols = mesh.shape["row"], mesh.shape["col"]
    order = chip_ring(rows)
    ahead = [(order[p], order[(p + 1) % rows]) for p in range(rows)]
    behind = [(target, source) for source, target in ahead]
    swap = [(0, 1), (1, 0)]
    half_rows = rows // cols
    scale = 1.0 / (9.0 * rows * cols)

    def local(activations, pseudo_grads, row_counts):
        row, col = lax.axis_index("row"), lax.axis_index("col")
        slots, act_width = activations.shape
        grad_width = pseudo_grads.shape[1]
        act_half, grad_half = act_width // cols, grad_width // cols
        act_block, grad_block = act_width // rows, grad_width // rows
        cut = act_block * 4 // 7 if act_block % 1792 == 0 else act_block
        rest = act_block - cut
        widths = [half_rows * cut, half_rows * rest + grad_half]
        if rest == 0:
            layouts = [[(1, 0, act_half)], [(0, 0, grad_half)]]
        else:
            layouts = [
                [(1, j * act_block, cut) for j in range(half_rows)],
                [(1, j * act_block + cut, rest) for j in range(half_rows)] + [(0, 0, grad_half)],
            ]
        chains = []
        for layout, width in zip(layouts, widths):
            used = sorted({source for source, _, _ in layout})
            frame = pltpu.VMEM((2 * slots, width), jnp.bfloat16)
            keep, send = pl.pallas_call(
                functools.partial(split_kernel, cols, [(used.index(n), start, wide) for n, start, wide in layout]),
                in_specs=[pl.BlockSpec(memory_space=pltpu.SMEM)] * 2
                + [pl.BlockSpec(memory_space=pltpu.VMEM)] * len(used),
                out_specs=[pl.BlockSpec(memory_space=pltpu.VMEM)] * 2,
                out_shape=[frame, frame],
            )(col[None], row_counts, *[(pseudo_grads, activations)[n] for n in used])
            chains.append([keep + lax.ppermute(send, "col", swap)])
        forward = [chain[0] for chain in chains]
        backward = list(forward)
        steps, halfway = [0] * len(chains), rows // 2
        sequence = [0, 1] * halfway
        mine = col == row // half_rows

        def block_of(part, pieces, block_row):
            cuts = [
                lax.dynamic_slice_in_dim(part, base + (block_row % half_rows) * size, size, 1) for base, size in pieces
            ]
            return cuts[0] if len(cuts) == 1 else jnp.concatenate(cuts, axis=1)

        def swapped(own):
            return own, lax.ppermute(own, "col", swap)

        def early_part(chain, pieces):
            return swapped(jnp.concatenate([block_of(part, pieces, row) for part in chain], axis=0))

        def left_part(early, late):
            return jnp.concatenate([jnp.where(mine, *early), jnp.where(mine, *late)], axis=0)

        first_pieces = [(0, cut)]
        second_pieces = [(0, rest), (half_rows * rest, grad_block)] if rest else [(0, grad_block)]
        previous, hold = (), []
        for k in sequence:
            chain, middle = chains[k], widths[k] // 2
            steps[k] += 1
            ahead_of, _ = lax.optimization_barrier((forward[k], previous))
            behind_of, _ = lax.optimization_barrier((backward[k], (previous, hold)))
            previous = forward[k]
            if steps[k] == halfway:
                ahead_of, behind_of = ahead_of[:, :middle], behind_of[:, middle:]
            forward[k] = lax.ppermute(ahead_of, "row", ahead)
            backward[k] = lax.ppermute(behind_of, "row", behind)
            if steps[k] < halfway:
                chain += [forward[k], backward[k]]
                latest = (forward[k], backward[k])
            elif k == 0:
                halves, _ = lax.optimization_barrier(((forward[k], backward[k]), latest))
                chain.append(jnp.concatenate(halves, axis=1))
                late = block_of(chain[-1], first_pieces, row)
                hold.append(late)
                left_first = left_part(early_part(chain[:-1], first_pieces), swapped(late))

        early_second = early_part(chains[1], second_pieces)
        if rest == 0:
            chains[1].append(jnp.concatenate((forward[1], backward[1]), axis=1))
            left_grad = left_part(early_second, swapped(block_of(chains[1][-1], second_pieces, row)))
            act_cov = gram(left_first, chains[0], scale, act_half // 256, 256)
            grad_cov = gram(left_grad, chains[1], scale, grad_half // 256, 256)
        else:
            first_part, second_part = (0, 0, cut, cut), (1, 0, rest, rest)
            grad_part = (1, half_rows * rest, grad_block, grad_block)
            act_shape, grad_shape = (act_block, act_half), (grad_block, grad_half)
            half_blocks = half_rows // 2

            def square(start, lefts, out, **more):
                parts = [(0, start * cut, cut, cut)]
                group = (0, cut, 2, parts, 0, 0, start * act_block, act_block, half_blocks)
                return tiles(scale, [group], lefts, [chains[0]], [act_shape], out, **more)

            act_cov, turned_first = square(0, [left_first], None, hand_on=True)
            halves, act_cov = lax.optimization_barrier(((forward[1], backward[1]), act_cov))
            chains[1].append(jnp.concatenate(halves, axis=1))
            left_second = left_part(early_second, swapped(block_of(chains[1][-1], second_pieces, row)))
            (act_cov,) = square(half_blocks, [turned_first], act_cov, ready=[True])
            act_cov, grad_cov = tiles(
                scale,
                [
                    (2, grad_block, 1, [grad_part], 1, 0, 0, grad_block, half_rows),
                    (1, rest, 2, [first_part, second_part], 0, cut, 0, act_block, half_rows),
                    (0, cut, 2, [second_part], 0, 0, cut, act_block, half_rows),
                ],
                [turned_first, left_second[:, :rest], left_second[:, rest:]],
                chains, [act_shape, grad_shape], act_cov, ready=[True, False, False],
            )
        return act_cov, grad_cov

    return jax.shard_map(
        local,
        mesh=mesh,
        in_specs=(
            P(("groups", "row", "col"), None),
            P(("groups", "row", "col"), None),
            P(("groups", "row", "col")),
        ),
        out_specs=(P(("groups", "row"), "col"), P(("groups", "row"), "col")),
        check_vma=False,
    )
```

```python
import functools

import jax
import jax.numpy as jnp
from jax import lax
from jax.experimental import pallas as pl
from jax.experimental.pallas import tpu as pltpu
from jax.sharding import PartitionSpec as P


SLOTS, PIECE = 4, 128


def chip_ring(rows):
    width = 2 if rows <= 8 else 4
    depth = rows // width
    order = [z * width for z in range(depth)]
    for step, z in enumerate(reversed(range(depth))):
        columns = range(1, width) if step % 2 == 0 else range(width - 1, 0, -1)
        order += [z * width + x for x in columns]
    return order


def gram_kernel(scale, left_ref, *refs):
    right_refs, out_ref, turned = refs[:-2], refs[-2], refs[-1]

    @pl.when(pl.program_id(0) == 0)
    def _():
        turned[...] = left_ref[...].T

    right = jnp.concatenate([ref[...] for ref in right_refs], axis=0)
    out_ref[...] = jnp.dot(turned[...], right, preferred_element_type=jnp.float32) * scale


def gram(left, rights, scale, steps, tile):
    tokens, height = left.shape
    return pl.pallas_call(
        functools.partial(gram_kernel, scale),
        grid=(steps,),
        in_specs=[pl.BlockSpec((tokens, height), lambda j: (0, 0))]
        + [pl.BlockSpec((part.shape[0], tile), lambda j: (0, j)) for part in rights],
        out_specs=pl.BlockSpec((height, tile), lambda j: (0, j)),
        out_shape=jax.ShapeDtypeStruct((height, steps * tile), jnp.float32),
        scratch_shapes=[pltpu.VMEM((height, tokens), jnp.bfloat16)],
        compiler_params=pltpu.CompilerParams(vmem_limit_bytes=32 * 1024 * 1024),
    )(left, *rights)


def tiles_kernel(scale, cut, rest, grad_cut, grad_rest, shards, *refs):
    first_left, second_left = refs[:2]
    first, second = refs[2 : 2 + shards], refs[2 + shards : 2 + 2 * shards]
    act_out, grad_out, turned, turned_grad, joined, buffer, sems = refs[2 + 2 * shards :]
    act_block, grad_block, blocks = cut + rest, grad_cut + grad_rest, first[0].shape[1] // (cut + grad_cut)
    grad_parts = [(first, blocks * cut, grad_cut, grad_cut), (second, blocks * rest, grad_rest, grad_rest)]
    groups = [(turned_grad, grad_parts, grad_block, grad_out, 0, grad_block, blocks)]
    groups.append((turned, [(second, 0, rest, rest)], rest, act_out, cut, act_block, blocks))
    start = 0
    for width in (cut // 2, cut // 4, cut // 4):
        groups.append((turned, [(first, start, cut, width)], width, act_out, start, act_block, blocks))
        start += width

    def copy(group, slot, j):
        left, _, width, out, column, stride, _ = group
        return pltpu.make_async_copy(
            buffer.at[slot, pl.ds(0, left.shape[0]), pl.ds(0, width)],
            out.at[:, pl.ds(pl.multiple_of(column + j * stride, 128), width)],
            sems.at[slot],
        )

    turned_grad[:grad_cut, :] = first_left[:, cut:].T
    turned_grad[grad_cut:, :] = second_left[:, rest:].T
    earlier = None
    for group in groups:

        def step(j, carry, group=group, earlier=earlier):
            left, parts, width = group[:3]
            height, slot, at = left.shape[0], lax.rem(j, SLOTS), 0
            for sources, start, apart, wide in parts:
                here = pl.ds(pl.multiple_of(start + j * apart, 128), wide)
                joined[:, at : at + wide] = jnp.concatenate([ref[:, here] for ref in sources], axis=0)
                at += wide

            @pl.when(j >= SLOTS)
            def _():
                copy(group, slot, 0).wait()

            if earlier is not None:

                @pl.when(j < SLOTS)
                def _():
                    copy(earlier, slot, 0).wait()

            for across in range(0, width, 256):
                right = joined[:, across : across + 256]
                for down in range(0, height, PIECE):
                    product = jnp.dot(left[down : down + PIECE, :], right, preferred_element_type=jnp.float32)
                    buffer[slot, down : down + PIECE, across : across + 256] = product * scale
            copy(group, slot, j).start()
            return carry

        lax.fori_loop(0, group[-1], step, 0)
        if earlier is None:
            turned[:cut, :] = first_left[:, :cut].T
            turned[cut:, :] = second_left[:, :rest].T
        earlier = group
    for slot in range(SLOTS):
        copy(earlier, slot, 0).wait()


def tiles(scale, cut, rest, grad_cut, first_left, second_left, chains):
    shards = len(chains[0])
    tokens, grad_rest = first_left.shape[0], second_left.shape[1] - rest
    blocks = chains[0][0].shape[1] // (cut + grad_cut)
    act_block, grad_block = cut + rest, grad_cut + grad_rest
    act_shape, grad_shape = (act_block, blocks * act_block), (grad_block, blocks * grad_block)
    area = act_shape[0] * act_shape[1] + grad_shape[0] * grad_shape[1]
    whole = pl.BlockSpec(memory_space=pltpu.VMEM)
    return pl.pallas_call(
        functools.partial(tiles_kernel, scale, cut, rest, grad_cut, grad_rest, shards),
        in_specs=[whole] * (2 + 2 * shards),
        out_specs=[pl.BlockSpec(memory_space=pl.ANY)] * 2,
        out_shape=[jax.ShapeDtypeStruct(shape, jnp.float32) for shape in (act_shape, grad_shape)],
        scratch_shapes=[
            pltpu.VMEM((act_block, tokens), jnp.bfloat16),
            pltpu.VMEM((grad_block, tokens), jnp.bfloat16),
            pltpu.VMEM((tokens, rest), jnp.bfloat16),
            pltpu.VMEM((SLOTS, act_block, rest), jnp.float32),
            pltpu.SemaphoreType.DMA((SLOTS,)),
        ],
        compiler_params=pltpu.CompilerParams(vmem_limit_bytes=40 * 1024 * 1024),
        cost_estimate=pl.CostEstimate(flops=2 * tokens * area, bytes_accessed=4 * area, transcendentals=0),
    )(first_left, second_left, *chains[0], *chains[1])


def split_kernel(halves, layouts, half_ref, count_ref, act_ref, grad_ref, *out_refs):
    slots = act_ref.shape[0]
    live = lax.broadcasted_iota(jnp.int32, (slots, 128), 0) < count_ref[0]
    for half in range(halves):
        for flip in (1, 0):

            @pl.when((half_ref[0] + flip) % halves == half)
            def _(half=half, flip=flip):
                for chain, layout in enumerate(layouts):
                    target = 0
                    for source, start, width in layout:
                        ref = (grad_ref, act_ref)[source]
                        first = half * (ref.shape[1] // halves) + start
                        values = ref[:, first : first + width]
                        mask = jnp.concatenate([live] * (width // 128), axis=1)
                        masked = jnp.where(mask, values, jnp.zeros_like(values))
                        own = (half + flip) % halves * slots
                        out_ref, columns = out_refs[2 * chain + flip], slice(target, target + width)
                        out_ref[own : own + slots, columns] = masked
                        other = slots - own
                        out_ref[other : other + slots, columns] = jnp.zeros_like(values)
                        target += width


def solution(mesh):
    rows, cols = mesh.shape["row"], mesh.shape["col"]
    order = chip_ring(rows)
    ahead = [(order[p], order[(p + 1) % rows]) for p in range(rows)]
    behind = [(target, source) for source, target in ahead]
    swap = [(0, 1), (1, 0)]
    half_rows = rows // cols
    scale = 1.0 / (9.0 * rows * cols)

    def local(activations, pseudo_grads, row_counts):
        row, col = lax.axis_index("row"), lax.axis_index("col")
        slots, act_width = activations.shape
        grad_width = pseudo_grads.shape[1]
        act_half, grad_half = act_width // cols, grad_width // cols
        act_block, grad_block = act_width // rows, grad_width // rows
        cut = act_block * 4 // 7 if act_block % 1792 == 0 else act_block
        rest = act_block - cut
        grad_cut = grad_block // 4 if rest else 0
        grad_rest = grad_block - grad_cut
        widths = [half_rows * (cut + grad_cut), half_rows * (rest + grad_rest)]
        if rest == 0:
            layouts = [[(1, 0, act_half)], [(0, 0, grad_half)]]
        else:
            layouts = [
                [(1, j * act_block, cut) for j in range(half_rows)]
                + [(0, j * grad_block, grad_cut) for j in range(half_rows)],
                [(1, j * act_block + cut, rest) for j in range(half_rows)]
                + [(0, j * grad_block + grad_cut, grad_rest) for j in range(half_rows)],
            ]
        pieces = pl.pallas_call(
            functools.partial(split_kernel, cols, layouts),
            in_specs=[pl.BlockSpec(memory_space=pltpu.SMEM)] * 2 + [pl.BlockSpec(memory_space=pltpu.VMEM)] * 2,
            out_specs=[pl.BlockSpec(memory_space=pltpu.VMEM)] * 4,
            out_shape=[pltpu.VMEM((2 * slots, width), jnp.bfloat16) for width in widths for _ in (0, 1)],
        )(col[None], row_counts, activations, pseudo_grads)
        chains = [[pieces[2 * k] + lax.ppermute(pieces[2 * k + 1], "col", swap)] for k in (0, 1)]
        forward = [chain[0] for chain in chains]
        backward = list(forward)
        steps, halfway = [0] * len(chains), rows // 2
        sequence = [0, 1] * halfway
        def left_part(chain, pieces):
            own = []
            for part in chain:
                cuts = [
                    lax.dynamic_slice_in_dim(part, base + (row % half_rows) * size, size, 1) for base, size in pieces
                ]
                own.append(cuts[0] if len(cuts) == 1 else jnp.concatenate(cuts, axis=1))
            groups = [jnp.concatenate(own[:-1], axis=0), own[-1]]
            mine = col == row // half_rows
            return jnp.concatenate([jnp.where(mine, g, lax.ppermute(g, "col", swap)) for g in groups], axis=0)

        previous = ()
        for k in sequence:
            chain = chains[k]
            steps[k] += 1
            ahead_of, _ = lax.optimization_barrier((forward[k], previous))
            behind_of, _ = lax.optimization_barrier((backward[k], previous))
            previous = forward[k]
            if steps[k] < halfway or k == 0:
                forward[k] = lax.ppermute(ahead_of, "row", ahead)
                chain.append(forward[k])
            if steps[k] < halfway or k == 1:
                backward[k] = lax.ppermute(behind_of, "row", behind)
                chain.append(backward[k])

        if rest == 0:
            left_first, left_grad = left_part(chains[0], [(0, cut)]), left_part(chains[1], [(0, grad_block)])
            act_cov = gram(left_first, chains[0], scale, act_half // 256, 256)
            grad_cov = gram(left_grad, chains[1], scale, grad_half // 256, 256)
        else:
            left_first = left_part(chains[0], [(0, cut), (half_rows * cut, grad_cut)])
            left_second = left_part(chains[1], [(0, rest), (half_rows * rest, grad_rest)])
            act_cov, grad_cov = tiles(scale, cut, rest, grad_cut, left_first, left_second, chains)
        return act_cov, grad_cov

    return jax.shard_map(
        local,
        mesh=mesh,
        in_specs=(
            P(("groups", "row", "col"), None),
            P(("groups", "row", "col"), None),
            P(("groups", "row", "col")),
        ),
        out_specs=(P(("groups", "row"), "col"), P(("groups", "row"), "col")),
        check_vma=False,
    )
```

```python
import functools

import jax
import jax.numpy as jnp
from jax import lax
from jax.experimental import pallas as pl
from jax.experimental.pallas import tpu as pltpu
from jax.sharding import PartitionSpec as P


SLOTS, CHUNK, PIECE = 4, 256, 128


def chip_ring(rows):
    width = 2 if rows <= 8 else 4
    depth = rows // width
    order = [z * width for z in range(depth)]
    for step, z in enumerate(reversed(range(depth))):
        columns = range(1, width) if step % 2 == 0 else range(width - 1, 0, -1)
        order += [z * width + x for x in columns]
    return order


def gram_kernel(scale, left_ref, *refs):
    right_refs, out_ref, turned = refs[:-2], refs[-2], refs[-1]

    @pl.when(pl.program_id(0) == 0)
    def _():
        turned[...] = left_ref[...].T

    right = jnp.concatenate([ref[...] for ref in right_refs], axis=0)
    out_ref[...] = jnp.dot(turned[...], right, preferred_element_type=jnp.float32) * scale


def gram(left, rights, scale, steps, tile):
    tokens, height = left.shape
    return pl.pallas_call(
        functools.partial(gram_kernel, scale),
        grid=(steps,),
        in_specs=[pl.BlockSpec((tokens, height), lambda j: (0, 0))]
        + [pl.BlockSpec((part.shape[0], tile), lambda j: (0, j)) for part in rights],
        out_specs=pl.BlockSpec((height, tile), lambda j: (0, j)),
        out_shape=jax.ShapeDtypeStruct((height, steps * tile), jnp.float32),
        scratch_shapes=[pltpu.VMEM((height, tokens), jnp.bfloat16)],
        compiler_params=pltpu.CompilerParams(vmem_limit_bytes=32 * 1024 * 1024),
    )(left, *rights)


def tiles_kernel(scale, groups, ready, lists, outs, aliased, *refs):
    left_refs, refs = refs[: len(ready)], refs[len(ready) :]
    sources = []
    for shards in lists:
        sources.append(refs[:shards])
        refs = refs[shards:]
    refs = refs[aliased:]
    out_refs, turned = refs[:outs], list(refs[outs:-3])
    joined, buffer, sems = refs[-3:]
    turned = [left_ref if done else turned.pop(0) for left_ref, done in zip(left_refs, ready)]

    def copy(group, slot, j, down=0, rows=None):
        _, height, (_, _, _, width), which, row, column, stride, _ = group
        rows = rows or height
        return pltpu.make_async_copy(
            buffer.at[slot, pl.ds(down, rows), pl.ds(0, width)],
            out_refs[which].at[pl.ds(row + down, rows), pl.ds(pl.multiple_of(column + j * stride, 128), width)],
            sems.at[slot],
        )

    earlier, done = None, [index for index, is_ready in enumerate(ready) if is_ready]
    for group in groups:
        left = group[0]
        if left not in done:
            done.append(left)
            turned[left][...] = left_refs[left][...].T

        def step(j, carry, group=group, earlier=earlier):
            left, height, (source, first, apart, width), _, _, _, _, _ = group
            slot = lax.rem(j, SLOTS)
            here = pl.ds(pl.multiple_of(first + j * apart, 128), width)
            joined[:, :width] = jnp.concatenate([ref[:, here] for ref in sources[source]], axis=0)

            @pl.when(j >= SLOTS)
            def _():
                copy(group, slot, 0).wait()

            if earlier is not None:

                @pl.when(j < SLOTS)
                def _():
                    copy(earlier, slot, 0).wait()

            for down in range(0, height, CHUNK):
                for across in range(0, width, 256):
                    right = joined[:, across : across + 256]
                    for at in range(down, down + CHUNK, PIECE):
                        rows = turned[left][at : at + PIECE, :]
                        product = jnp.dot(rows, right, preferred_element_type=jnp.float32)
                        buffer[slot, at : at + PIECE, across : across + 256] = product * scale
                copy(group, slot, j, down, CHUNK).start()
            return carry

        lax.fori_loop(0, group[-1], step, 0)
        earlier = group
    for slot in range(SLOTS):
        copy(earlier, slot, 0).wait()


def tiles(scale, groups, lefts, lists, out_shapes, out=None, ready=(), hand_on=False):
    ready = tuple(ready) or (False,) * len(lefts)
    tokens = lists[0][0].shape[0] * len(lists[0])
    whole, anywhere = pl.BlockSpec(memory_space=pltpu.VMEM), pl.BlockSpec(memory_space=pl.ANY)
    operands = [*lefts, *[part for parts in lists for part in parts]]
    specs, aliases = [whole] * len(operands), {}
    if out is not None:
        aliases = {len(operands): 0}
        operands.append(out)
        specs.append(anywhere)
    area = sum(g[1] * g[2][3] * g[7] for g in groups)
    turned = [(left.shape[1], tokens) for left, done in zip(lefts, ready) if not done]
    results = [jax.ShapeDtypeStruct(shape, jnp.float32) for shape in out_shapes]
    result_specs = [anywhere] * len(results)
    if hand_on:
        results.append(pltpu.VMEM(turned[0], jnp.bfloat16))
        result_specs.append(whole)
    return pl.pallas_call(
        functools.partial(
            tiles_kernel, scale, groups, ready, [len(parts) for parts in lists], len(out_shapes), len(aliases)
        ),
        in_specs=specs,
        out_specs=result_specs,
        out_shape=results,
        scratch_shapes=[pltpu.VMEM(shape, jnp.bfloat16) for shape in turned[int(hand_on) :]]
        + [
            pltpu.VMEM((tokens, max(g[2][3] for g in groups)), jnp.bfloat16),
            pltpu.VMEM((SLOTS, max(g[1] for g in groups), max(g[2][3] for g in groups)), jnp.float32),
            pltpu.SemaphoreType.DMA((SLOTS,)),
        ],
        input_output_aliases=aliases,
        compiler_params=pltpu.CompilerParams(vmem_limit_bytes=32 * 1024 * 1024),
        cost_estimate=pl.CostEstimate(flops=2 * tokens * area, bytes_accessed=4 * area, transcendentals=0),
    )(*operands)


def split_kernel(halves, layouts, half_ref, count_ref, act_ref, grad_ref, *out_refs):
    slots = act_ref.shape[0]
    live = lax.broadcasted_iota(jnp.int32, (slots, 128), 0) < count_ref[0]
    for half in range(halves):
        for flip in (1, 0):

            @pl.when((half_ref[0] + flip) % halves == half)
            def _(half=half, flip=flip):
                for chain, layout in enumerate(layouts):
                    target = 0
                    for source, start, width in layout:
                        ref = (grad_ref, act_ref)[source]
                        first = half * (ref.shape[1] // halves) + start
                        values = ref[:, first : first + width]
                        mask = jnp.concatenate([live] * (width // 128), axis=1)
                        masked = jnp.where(mask, values, jnp.zeros_like(values))
                        own = (half + flip) % halves * slots
                        out_ref, columns = out_refs[2 * chain + flip], slice(target, target + width)
                        out_ref[own : own + slots, columns] = masked
                        other = slots - own
                        out_ref[other : other + slots, columns] = jnp.zeros_like(values)
                        target += width


def solution(mesh):
    rows, cols = mesh.shape["row"], mesh.shape["col"]
    order = chip_ring(rows)
    ahead = [(order[p], order[(p + 1) % rows]) for p in range(rows)]
    behind = [(target, source) for source, target in ahead]
    swap = [(0, 1), (1, 0)]
    half_rows = rows // cols
    scale = 1.0 / (9.0 * rows * cols)

    def local(activations, pseudo_grads, row_counts):
        row, col = lax.axis_index("row"), lax.axis_index("col")
        slots, act_width = activations.shape
        grad_width = pseudo_grads.shape[1]
        act_half, grad_half = act_width // cols, grad_width // cols
        act_block, grad_block = act_width // rows, grad_width // rows
        cut = act_block * 4 // 7 if act_block % 1792 == 0 else act_block
        rest = act_block - cut
        widths = [half_rows * cut, half_rows * rest + grad_half]
        if rest == 0:
            layouts = [[(1, 0, act_half)], [(0, 0, grad_half)]]
        else:
            layouts = [
                [(1, j * act_block, cut) for j in range(half_rows)],
                [(1, j * act_block + cut, rest) for j in range(half_rows)] + [(0, 0, grad_half)],
            ]
        pieces = pl.pallas_call(
            functools.partial(split_kernel, cols, layouts),
            in_specs=[pl.BlockSpec(memory_space=pltpu.SMEM)] * 2 + [pl.BlockSpec(memory_space=pltpu.VMEM)] * 2,
            out_specs=[pl.BlockSpec(memory_space=pltpu.VMEM)] * 4,
            out_shape=[pltpu.VMEM((2 * slots, width), jnp.bfloat16) for width in widths for _ in (0, 1)],
        )(col[None], row_counts, activations, pseudo_grads)
        chains = [[pieces[2 * k] + lax.ppermute(pieces[2 * k + 1], "col", swap)] for k in (0, 1)]
        forward = [chain[0] for chain in chains]
        backward = list(forward)
        steps, halfway = [0] * len(chains), rows // 2
        sequence = [0, 1] * halfway
        def left_part(chain, pieces, hold=None):
            own = []
            for part in chain:
                cuts = [
                    lax.dynamic_slice_in_dim(part, base + (row % half_rows) * size, size, 1) for base, size in pieces
                ]
                own.append(cuts[0] if len(cuts) == 1 else jnp.concatenate(cuts, axis=1))
            groups = [jnp.concatenate(own[:-1], axis=0), own[-1]]
            mine = col == row // half_rows
            if hold is not None:
                hold.append(groups[1])
            return jnp.concatenate([jnp.where(mine, g, lax.ppermute(g, "col", swap)) for g in groups], axis=0)

        previous, hold, left_first = (), [], None
        for k in sequence:
            chain, middle = chains[k], widths[k] // 2
            steps[k] += 1
            final = steps[k] == halfway
            ahead_of, _ = lax.optimization_barrier((forward[k], previous))
            behind_of, _ = lax.optimization_barrier((backward[k], (previous, hold)))
            previous = forward[k]
            if final:
                ahead_of, behind_of = ahead_of[:, :middle], behind_of[:, middle:]
            forward[k] = lax.ppermute(ahead_of, "row", ahead)
            backward[k] = lax.ppermute(behind_of, "row", behind)
            if not final:
                chain += [forward[k], backward[k]]
                latest = (forward[k], backward[k])
            elif k == 0:
                last_first, _ = lax.optimization_barrier(((forward[k], backward[k]), latest))
                chain.append(jnp.concatenate(last_first, axis=1))
                left_first = left_part(chain, [(0, cut)], hold)

        act_shape, grad_shape = (act_block, act_half), (grad_block, grad_half)
        if rest == 0:
            chains[1].append(jnp.concatenate((forward[1], backward[1]), axis=1))
            left_grad = left_part(chains[1], [(0, grad_block)])
            act_cov = gram(left_first, chains[0], scale, act_half // 256, 256)
            grad_cov = gram(left_grad, chains[1], scale, grad_half // 256, 256)
        else:
            grad_first = half_rows * rest
            first_part, second_part = (0, 0, cut, cut), (1, 0, rest, rest)
            grad_part = (1, grad_first, grad_block, grad_block)

            def square(part, lefts, out, **more):
                starts = [part * cut // 2, part * cut // 2 + cut // 4]
                groups = [(0, cut, (0, at, cut, cut // 4), 0, 0, at, act_block, half_rows) for at in starts]
                return tiles(scale, groups, lefts, [chains[0]], [act_shape], out, **more)

            act_cov, turned_first = square(0, [left_first], None, hand_on=True)
            last_second, act_cov = lax.optimization_barrier(((forward[1], backward[1]), act_cov))
            chains[1].append(jnp.concatenate(last_second, axis=1))
            left_second = left_part(chains[1], [(0, rest), (grad_first, grad_block)])
            (act_cov,) = square(1, [turned_first], act_cov, ready=[True])
            act_cov, grad_cov = tiles(
                scale,
                [
                    (2, grad_block, grad_part, 1, 0, 0, grad_block, half_rows),
                    (0, cut, second_part, 0, 0, cut, act_block, half_rows),
                    (1, rest, first_part, 0, cut, 0, act_block, half_rows),
                    (1, rest, second_part, 0, cut, cut, act_block, half_rows),
                ],
                [turned_first, left_second[:, :rest], left_second[:, rest:]],
                chains, [act_shape, grad_shape], act_cov, ready=[True, False, False],
            )
        return act_cov, grad_cov

    return jax.shard_map(
        local,
        mesh=mesh,
        in_specs=(
            P(("groups", "row", "col"), None),
            P(("groups", "row", "col"), None),
            P(("groups", "row", "col")),
        ),
        out_specs=(P(("groups", "row"), "col"), P(("groups", "row"), "col")),
        check_vma=False,
    )
```

```python
import functools

import jax
import jax.numpy as jnp
from jax import lax
from jax.experimental import pallas as pl
from jax.experimental.pallas import tpu as pltpu
from jax.sharding import PartitionSpec as P


SLOTS, CHUNK, PIECE = 4, 256, 128


def chip_ring(rows):
    width = 2 if rows <= 8 else 4
    depth = rows // width
    order = [z * width for z in range(depth)]
    for step, z in enumerate(reversed(range(depth))):
        columns = range(1, width) if step % 2 == 0 else range(width - 1, 0, -1)
        order += [z * width + x for x in columns]
    return order


def gram_kernel(scale, left_ref, *refs):
    right_refs, out_ref, turned = refs[:-2], refs[-2], refs[-1]

    @pl.when(pl.program_id(0) == 0)
    def _():
        turned[...] = left_ref[...].T

    right = jnp.concatenate([ref[...] for ref in right_refs], axis=0)
    out_ref[...] = jnp.dot(turned[...], right, preferred_element_type=jnp.float32) * scale


def gram(left, rights, scale, steps, tile):
    tokens, height = left.shape
    return pl.pallas_call(
        functools.partial(gram_kernel, scale),
        grid=(steps,),
        in_specs=[pl.BlockSpec((tokens, height), lambda j: (0, 0))]
        + [pl.BlockSpec((part.shape[0], tile), lambda j: (0, j)) for part in rights],
        out_specs=pl.BlockSpec((height, tile), lambda j: (0, j)),
        out_shape=jax.ShapeDtypeStruct((height, steps * tile), jnp.float32),
        scratch_shapes=[pltpu.VMEM((height, tokens), jnp.bfloat16)],
        compiler_params=pltpu.CompilerParams(vmem_limit_bytes=32 * 1024 * 1024),
    )(left, *rights)


def tiles_kernel(scale, groups, ready, lists, outs, aliased, *refs):
    left_refs, refs = refs[: len(ready)], refs[len(ready) :]
    sources = []
    for shards in lists:
        sources.append(refs[:shards])
        refs = refs[shards:]
    refs = refs[aliased:]
    out_refs, turned = refs[:outs], list(refs[outs:-3])
    joined, buffer, sems = refs[-3:]
    turned = [left_ref if done else turned.pop(0) for left_ref, done in zip(left_refs, ready)]

    def copy(group, slot, j, down=0, rows=None):
        _, height, (_, _, _, width), which, row, column, stride, _ = group
        rows = rows or height
        return pltpu.make_async_copy(
            buffer.at[slot, pl.ds(down, rows), pl.ds(0, width)],
            out_refs[which].at[pl.ds(row + down, rows), pl.ds(pl.multiple_of(column + j * stride, 128), width)],
            sems.at[slot],
        )

    done = [index for index, is_ready in enumerate(ready) if is_ready]
    banks = buffer.shape[0] // SLOTS
    for number, group in enumerate(groups):
        left = group[0]
        if left not in done:
            done.append(left)
            turned[left][...] = left_refs[left][...].T
        earlier = groups[number - banks] if number >= banks else None

        def step(j, carry, group=group, earlier=earlier, bank=number % banks):
            left, height, (source, first, apart, width), _, _, _, _, _ = group
            slot = bank * SLOTS + j
            here = pl.ds(pl.multiple_of(first + j * apart, 128), width)
            joined[:, :width] = jnp.concatenate([ref[:, here] for ref in sources[source]], axis=0)
            if earlier is not None:
                copy(earlier, slot, j).wait()
            for down in range(0, height, CHUNK):
                for across in range(0, width, 256):
                    right = joined[:, across : across + 256]
                    for at in range(down, down + CHUNK, PIECE):
                        rows = turned[left][at : at + PIECE, :]
                        product = jnp.dot(rows, right, preferred_element_type=jnp.float32)
                        buffer[slot, at : at + PIECE, across : across + 256] = product * scale
                copy(group, slot, j, down, CHUNK).start()
            return carry

        lax.fori_loop(0, SLOTS, step, 0)
    for number in range(max(0, len(groups) - banks), len(groups)):
        for j in range(SLOTS):
            copy(groups[number], number % banks * SLOTS + j, j).wait()


def tiles(scale, groups, lefts, lists, out_shapes, out=None, ready=(), hand_on=False, banks=1):
    ready = tuple(ready) or (False,) * len(lefts)
    tokens = lists[0][0].shape[0] * len(lists[0])
    whole, anywhere = pl.BlockSpec(memory_space=pltpu.VMEM), pl.BlockSpec(memory_space=pl.ANY)
    operands = [*lefts, *[part for parts in lists for part in parts]]
    specs, aliases = [whole] * len(operands), {}
    if out is not None:
        aliases = {len(operands): 0}
        operands.append(out)
        specs.append(anywhere)
    area = sum(g[1] * g[2][3] * g[7] for g in groups)
    turned = [(left.shape[1], tokens) for left, done in zip(lefts, ready) if not done]
    results = [jax.ShapeDtypeStruct(shape, jnp.float32) for shape in out_shapes]
    result_specs = [anywhere] * len(results)
    if hand_on:
        results.append(pltpu.VMEM(turned[0], jnp.bfloat16))
        result_specs.append(whole)
    return pl.pallas_call(
        functools.partial(
            tiles_kernel, scale, groups, ready, [len(parts) for parts in lists], len(out_shapes), len(aliases)
        ),
        in_specs=specs,
        out_specs=result_specs,
        out_shape=results,
        scratch_shapes=[pltpu.VMEM(shape, jnp.bfloat16) for shape in turned[int(hand_on) :]]
        + [
            pltpu.VMEM((tokens, max(g[2][3] for g in groups)), jnp.bfloat16),
            pltpu.VMEM((banks * SLOTS, max(g[1] for g in groups), max(g[2][3] for g in groups)), jnp.float32),
            pltpu.SemaphoreType.DMA((banks * SLOTS,)),
        ],
        input_output_aliases=aliases,
        compiler_params=pltpu.CompilerParams(vmem_limit_bytes=32 * 1024 * 1024),
        cost_estimate=pl.CostEstimate(flops=2 * tokens * area, bytes_accessed=4 * area, transcendentals=0),
    )(*operands)


def split_kernel(halves, layouts, half_ref, count_ref, act_ref, grad_ref, *out_refs):
    slots = act_ref.shape[0]
    live = lax.broadcasted_iota(jnp.int32, (slots, 128), 0) < count_ref[0]
    for half in range(halves):
        for flip in (1, 0):

            @pl.when((half_ref[0] + flip) % halves == half)
            def _(half=half, flip=flip):
                for chain, layout in enumerate(layouts):
                    target = 0
                    for source, start, width in layout:
                        ref = (grad_ref, act_ref)[source]
                        first = half * (ref.shape[1] // halves) + start
                        values = ref[:, first : first + width]
                        mask = jnp.concatenate([live] * (width // 128), axis=1)
                        masked = jnp.where(mask, values, jnp.zeros_like(values))
                        own = (half + flip) % halves * slots
                        out_ref, columns = out_refs[2 * chain + flip], slice(target, target + width)
                        out_ref[own : own + slots, columns] = masked
                        other = slots - own
                        out_ref[other : other + slots, columns] = jnp.zeros_like(values)
                        target += width


def solution(mesh):
    rows, cols = mesh.shape["row"], mesh.shape["col"]
    order = chip_ring(rows)
    ahead = [(order[p], order[(p + 1) % rows]) for p in range(rows)]
    behind = [(target, source) for source, target in ahead]
    swap = [(0, 1), (1, 0)]
    half_rows = rows // cols
    scale = 1.0 / (9.0 * rows * cols)

    def local(activations, pseudo_grads, row_counts):
        row, col = lax.axis_index("row"), lax.axis_index("col")
        slots, act_width = activations.shape
        grad_width = pseudo_grads.shape[1]
        act_half, grad_half = act_width // cols, grad_width // cols
        act_block, grad_block = act_width // rows, grad_width // rows
        cut = act_block * 4 // 7 if act_block % 1792 == 0 and half_rows == SLOTS else act_block
        rest = act_block - cut
        widths = [half_rows * cut, half_rows * rest + grad_half]
        if rest == 0:
            layouts = [[(1, 0, act_half)], [(0, 0, grad_half)]]
        else:
            layouts = [
                [(1, j * act_block, cut) for j in range(half_rows)],
                [(1, j * act_block + cut, rest) for j in range(half_rows)] + [(0, 0, grad_half)],
            ]
        pieces = pl.pallas_call(
            functools.partial(split_kernel, cols, layouts),
            in_specs=[pl.BlockSpec(memory_space=pltpu.SMEM)] * 2 + [pl.BlockSpec(memory_space=pltpu.VMEM)] * 2,
            out_specs=[pl.BlockSpec(memory_space=pltpu.VMEM)] * 4,
            out_shape=[pltpu.VMEM((2 * slots, width), jnp.bfloat16) for width in widths for _ in (0, 1)],
        )(col[None], row_counts, activations, pseudo_grads)
        chains = [[pieces[2 * k] + lax.ppermute(pieces[2 * k + 1], "col", swap)] for k in (0, 1)]
        forward = [chain[0] for chain in chains]
        backward = list(forward)
        steps, halfway = [0] * len(chains), rows // 2
        sequence = [0, 1] * halfway
        def left_part(chain, pieces, hold=None):
            own = []
            for part in chain:
                cuts = [
                    lax.dynamic_slice_in_dim(part, base + (row % half_rows) * size, size, 1) for base, size in pieces
                ]
                own.append(cuts[0] if len(cuts) == 1 else jnp.concatenate(cuts, axis=1))
            groups = [jnp.concatenate(own[:-1], axis=0), own[-1]]
            mine = col == row // half_rows
            if hold is not None:
                hold.append(groups[1])
            return jnp.concatenate([jnp.where(mine, g, lax.ppermute(g, "col", swap)) for g in groups], axis=0)

        previous, hold, left_first = (), [], None
        for k in sequence:
            chain, middle = chains[k], widths[k] // 2
            steps[k] += 1
            final = steps[k] == halfway
            ahead_of, _ = lax.optimization_barrier((forward[k], previous))
            behind_of, _ = lax.optimization_barrier((backward[k], (previous, hold)))
            previous = forward[k]
            if final:
                ahead_of, behind_of = ahead_of[:, :middle], behind_of[:, middle:]
            forward[k] = lax.ppermute(ahead_of, "row", ahead)
            backward[k] = lax.ppermute(behind_of, "row", behind)
            if not final:
                chain += [forward[k], backward[k]]
                latest = (forward[k], backward[k])
            elif k == 0:
                last_first, _ = lax.optimization_barrier(((forward[k], backward[k]), latest))
                chain.append(jnp.concatenate(last_first, axis=1))
                left_first = left_part(chain, [(0, cut)], hold)

        act_shape, grad_shape = (act_block, act_half), (grad_block, grad_half)
        if rest == 0:
            chains[1].append(jnp.concatenate((forward[1], backward[1]), axis=1))
            left_grad = left_part(chains[1], [(0, grad_block)])
            act_cov = gram(left_first, chains[0], scale, act_half // 256, 256)
            grad_cov = gram(left_grad, chains[1], scale, grad_half // 256, 256)
        else:
            grad_first = half_rows * rest
            first_part, second_part = (0, 0, cut, cut), (1, 0, rest, rest)
            grad_part = (1, grad_first, grad_block, grad_block)

            def square(part, lefts, out, **more):
                starts = [part * cut // 2, part * cut // 2 + cut // 4]
                groups = [(0, cut, (0, at, cut, cut // 4), 0, 0, at, act_block, half_rows) for at in starts]
                return tiles(scale, groups, lefts, [chains[0]], [act_shape], out, banks=2, **more)

            act_cov, turned_first = square(0, [left_first], None, hand_on=True)
            last_second, act_cov = lax.optimization_barrier(((forward[1], backward[1]), act_cov))
            chains[1].append(jnp.concatenate(last_second, axis=1))
            left_second = left_part(chains[1], [(0, rest), (grad_first, grad_block)])
            (act_cov,) = square(1, [turned_first], act_cov, ready=[True])
            act_cov, grad_cov = tiles(
                scale,
                [
                    (2, grad_block, grad_part, 1, 0, 0, grad_block, half_rows),
                    (0, cut, second_part, 0, 0, cut, act_block, half_rows),
                    (1, rest, first_part, 0, cut, 0, act_block, half_rows),
                    (1, rest, second_part, 0, cut, cut, act_block, half_rows),
                ],
                [turned_first, left_second[:, :rest], left_second[:, rest:]],
                chains, [act_shape, grad_shape], act_cov, ready=[True, False, False],
            )
        return act_cov, grad_cov

    return jax.shard_map(
        local,
        mesh=mesh,
        in_specs=(
            P(("groups", "row", "col"), None),
            P(("groups", "row", "col"), None),
            P(("groups", "row", "col")),
        ),
        out_specs=(P(("groups", "row"), "col"), P(("groups", "row"), "col")),
        check_vma=False,
    )
```

```python
import functools

import jax
import jax.numpy as jnp
from jax import lax
from jax.experimental import pallas as pl
from jax.experimental.pallas import tpu as pltpu
from jax.sharding import PartitionSpec as P


SLOTS, CHUNK, PIECE = 4, 256, 128


def chip_ring(rows):
    width = 2 if rows <= 8 else 4
    depth = rows // width
    order = [z * width for z in range(depth)]
    for step, z in enumerate(reversed(range(depth))):
        columns = range(1, width) if step % 2 == 0 else range(width - 1, 0, -1)
        order += [z * width + x for x in columns]
    return order


def gram_kernel(scale, left_ref, *refs):
    right_refs, out_ref, turned = refs[:-2], refs[-2], refs[-1]

    @pl.when(pl.program_id(0) == 0)
    def _():
        turned[...] = left_ref[...].T

    right = jnp.concatenate([ref[...] for ref in right_refs], axis=0)
    out_ref[...] = jnp.dot(turned[...], right, preferred_element_type=jnp.float32) * scale


def gram(left, rights, scale, steps, tile):
    tokens, height = left.shape
    return pl.pallas_call(
        functools.partial(gram_kernel, scale),
        grid=(steps,),
        in_specs=[pl.BlockSpec((tokens, height), lambda j: (0, 0))]
        + [pl.BlockSpec((part.shape[0], tile), lambda j: (0, j)) for part in rights],
        out_specs=pl.BlockSpec((height, tile), lambda j: (0, j)),
        out_shape=jax.ShapeDtypeStruct((height, steps * tile), jnp.float32),
        scratch_shapes=[pltpu.VMEM((height, tokens), jnp.bfloat16)],
        compiler_params=pltpu.CompilerParams(vmem_limit_bytes=32 * 1024 * 1024),
    )(left, *rights)


def tiles_kernel(scale, groups, ready, lists, outs, aliased, *refs):
    left_refs, refs = refs[: len(ready)], refs[len(ready) :]
    sources = []
    for shards in lists:
        sources.append(refs[:shards])
        refs = refs[shards:]
    refs = refs[aliased:]
    out_refs, turned = refs[:outs], list(refs[outs:-3])
    joined, buffer, sems = refs[-3:]
    turned = [left_ref if done else turned.pop(0) for left_ref, done in zip(left_refs, ready)]

    def copy(group, slot, j, down=0, rows=None):
        _, height, (_, _, _, width), which, row, column, stride, _ = group
        rows = rows or height
        return pltpu.make_async_copy(
            buffer.at[slot, pl.ds(down, rows), pl.ds(0, width)],
            out_refs[which].at[pl.ds(row + down, rows), pl.ds(pl.multiple_of(column + j * stride, 128), width)],
            sems.at[slot],
        )

    done = [index for index, is_ready in enumerate(ready) if is_ready]
    banks = buffer.shape[0] // SLOTS
    for number, group in enumerate(groups):
        left = group[0]
        if left not in done:
            done.append(left)
            turned[left][...] = left_refs[left][...].T
        earlier = groups[number - banks] if number >= banks else None

        def step(j, carry, group=group, earlier=earlier, bank=number % banks):
            left, height, (source, first, apart, width), _, _, _, _, _ = group
            slot = bank * SLOTS + j
            here = pl.ds(pl.multiple_of(first + j * apart, 128), width)
            joined[:, :width] = jnp.concatenate([ref[:, here] for ref in sources[source]], axis=0)
            if earlier is not None:
                copy(earlier, slot, j).wait()
            for down in range(0, height, CHUNK):
                for across in range(0, width, 256):
                    right = joined[:, across : across + 256]
                    for at in range(down, down + CHUNK, PIECE):
                        rows = turned[left][at : at + PIECE, :]
                        product = jnp.dot(rows, right, preferred_element_type=jnp.float32)
                        buffer[slot, at : at + PIECE, across : across + 256] = product * scale
                copy(group, slot, j, down, CHUNK).start()
            return carry

        lax.fori_loop(0, SLOTS, step, 0)
    for number in range(max(0, len(groups) - banks), len(groups)):
        for j in range(SLOTS):
            copy(groups[number], number % banks * SLOTS + j, j).wait()


def tiles(scale, groups, lefts, lists, out_shapes, out=None, ready=(), hand_on=False, banks=1):
    ready = tuple(ready) or (False,) * len(lefts)
    tokens = lists[0][0].shape[0] * len(lists[0])
    whole, anywhere = pl.BlockSpec(memory_space=pltpu.VMEM), pl.BlockSpec(memory_space=pl.ANY)
    operands = [*lefts, *[part for parts in lists for part in parts]]
    specs, aliases = [whole] * len(operands), {}
    if out is not None:
        aliases = {len(operands): 0}
        operands.append(out)
        specs.append(anywhere)
    area = sum(g[1] * g[2][3] * g[7] for g in groups)
    turned = [(left.shape[1], tokens) for left, done in zip(lefts, ready) if not done]
    results = [jax.ShapeDtypeStruct(shape, jnp.float32) for shape in out_shapes]
    result_specs = [anywhere] * len(results)
    if hand_on:
        results.append(pltpu.VMEM(turned[0], jnp.bfloat16))
        result_specs.append(whole)
    return pl.pallas_call(
        functools.partial(
            tiles_kernel, scale, groups, ready, [len(parts) for parts in lists], len(out_shapes), len(aliases)
        ),
        in_specs=specs,
        out_specs=result_specs,
        out_shape=results,
        scratch_shapes=[pltpu.VMEM(shape, jnp.bfloat16) for shape in turned[int(hand_on) :]]
        + [
            pltpu.VMEM((tokens, max(g[2][3] for g in groups)), jnp.bfloat16),
            pltpu.VMEM((banks * SLOTS, max(g[1] for g in groups), max(g[2][3] for g in groups)), jnp.float32),
            pltpu.SemaphoreType.DMA((banks * SLOTS,)),
        ],
        input_output_aliases=aliases,
        compiler_params=pltpu.CompilerParams(vmem_limit_bytes=32 * 1024 * 1024),
        cost_estimate=pl.CostEstimate(flops=2 * tokens * area, bytes_accessed=4 * area, transcendentals=0),
    )(*operands)


def split_kernel(halves, layouts, half_ref, count_ref, act_ref, grad_ref, *out_refs):
    slots = act_ref.shape[0]
    own = half_ref[0] * slots
    position = lax.broadcasted_iota(jnp.int32, (halves * slots, 128), 0)
    live = (position >= own) & (position < own + count_ref[0])
    for half in range(halves):
        for flip in (1, 0):

            @pl.when((half_ref[0] + flip) % halves == half)
            def _(half=half, flip=flip):
                for chain, layout in enumerate(layouts):
                    target = 0
                    for source, start, width in layout:
                        ref = (grad_ref, act_ref)[source]
                        first = half * (ref.shape[1] // halves) + start
                        values = jnp.concatenate([ref[:, first : first + width]] * halves, axis=0)
                        mask = jnp.concatenate([live] * (width // 128), axis=1)
                        out_refs[2 * chain + flip][:, target : target + width] = jnp.where(
                            mask, values, jnp.zeros_like(values)
                        )
                        target += width


def solution(mesh):
    rows, cols = mesh.shape["row"], mesh.shape["col"]
    order = chip_ring(rows)
    ahead = [(order[p], order[(p + 1) % rows]) for p in range(rows)]
    behind = [(target, source) for source, target in ahead]
    swap = [(0, 1), (1, 0)]
    half_rows = rows // cols
    scale = 1.0 / (9.0 * rows * cols)

    def local(activations, pseudo_grads, row_counts):
        row, col = lax.axis_index("row"), lax.axis_index("col")
        slots, act_width = activations.shape
        grad_width = pseudo_grads.shape[1]
        act_half, grad_half = act_width // cols, grad_width // cols
        act_block, grad_block = act_width // rows, grad_width // rows
        cut = act_block * 4 // 7 if act_block % 1792 == 0 and half_rows == SLOTS else act_block
        rest = act_block - cut
        widths = [half_rows * cut, half_rows * rest + grad_half]
        if rest == 0:
            layouts = [[(1, 0, act_half)], [(0, 0, grad_half)]]
        else:
            layouts = [
                [(1, j * act_block, cut) for j in range(half_rows)],
                [(1, j * act_block + cut, rest) for j in range(half_rows)] + [(0, 0, grad_half)],
            ]
        pieces = pl.pallas_call(
            functools.partial(split_kernel, cols, layouts),
            in_specs=[pl.BlockSpec(memory_space=pltpu.SMEM)] * 2 + [pl.BlockSpec(memory_space=pltpu.VMEM)] * 2,
            out_specs=[pl.BlockSpec(memory_space=pltpu.VMEM)] * 4,
            out_shape=[pltpu.VMEM((2 * slots, width), jnp.bfloat16) for width in widths for _ in (0, 1)],
        )(col[None], row_counts, activations, pseudo_grads)
        chains = [[pieces[2 * k] + lax.ppermute(pieces[2 * k + 1], "col", swap)] for k in (0, 1)]
        forward = [chain[0] for chain in chains]
        backward = list(forward)
        steps, halfway = [0] * len(chains), rows // 2
        sequence = [0, 1] * halfway
        def left_part(chain, pieces, hold=None):
            own = []
            for part in chain:
                cuts = [
                    lax.dynamic_slice_in_dim(part, base + (row % half_rows) * size, size, 1) for base, size in pieces
                ]
                own.append(cuts[0] if len(cuts) == 1 else jnp.concatenate(cuts, axis=1))
            groups = [jnp.concatenate(own[:-1], axis=0), own[-1]]
            mine = col == row // half_rows
            if hold is not None:
                hold.append(groups[1])
            return jnp.concatenate([jnp.where(mine, g, lax.ppermute(g, "col", swap)) for g in groups], axis=0)

        previous, hold, left_first = (), [], None
        for k in sequence:
            chain, middle = chains[k], widths[k] // 2
            steps[k] += 1
            final = steps[k] == halfway
            ahead_of, _ = lax.optimization_barrier((forward[k], previous))
            behind_of, _ = lax.optimization_barrier((backward[k], (previous, hold)))
            previous = forward[k]
            if final:
                ahead_of, behind_of = ahead_of[:, :middle], behind_of[:, middle:]
            forward[k] = lax.ppermute(ahead_of, "row", ahead)
            backward[k] = lax.ppermute(behind_of, "row", behind)
            if not final:
                chain += [forward[k], backward[k]]
                latest = (forward[k], backward[k])
            elif k == 0:
                last_first, _ = lax.optimization_barrier(((forward[k], backward[k]), latest))
                chain.append(jnp.concatenate(last_first, axis=1))
                left_first = left_part(chain, [(0, cut)], hold)

        act_shape, grad_shape = (act_block, act_half), (grad_block, grad_half)
        if rest == 0:
            chains[1].append(jnp.concatenate((forward[1], backward[1]), axis=1))
            left_grad = left_part(chains[1], [(0, grad_block)])
            act_cov = gram(left_first, chains[0], scale, act_half // 256, 256)
            grad_cov = gram(left_grad, chains[1], scale, grad_half // 256, 256)
        else:
            grad_first = half_rows * rest
            first_part, second_part = (0, 0, cut, cut), (1, 0, rest, rest)
            grad_part = (1, grad_first, grad_block, grad_block)

            def square(part, lefts, out, **more):
                starts = [part * cut // 2, part * cut // 2 + cut // 4]
                groups = [(0, cut, (0, at, cut, cut // 4), 0, 0, at, act_block, half_rows) for at in starts]
                return tiles(scale, groups, lefts, [chains[0]], [act_shape], out, banks=2, **more)

            act_cov, turned_first = square(0, [left_first], None, hand_on=True)
            last_second, act_cov = lax.optimization_barrier(((forward[1], backward[1]), act_cov))
            chains[1].append(jnp.concatenate(last_second, axis=1))
            left_second = left_part(chains[1], [(0, rest), (grad_first, grad_block)])
            (act_cov,) = square(1, [turned_first], act_cov, ready=[True])
            act_cov, grad_cov = tiles(
                scale,
                [
                    (2, grad_block, grad_part, 1, 0, 0, grad_block, half_rows),
                    (0, cut, second_part, 0, 0, cut, act_block, half_rows),
                    (1, rest, first_part, 0, cut, 0, act_block, half_rows),
                    (1, rest, second_part, 0, cut, cut, act_block, half_rows),
                ],
                [turned_first, left_second[:, :rest], left_second[:, rest:]],
                chains, [act_shape, grad_shape], act_cov, ready=[True, False, False],
            )
        return act_cov, grad_cov

    return jax.shard_map(
        local,
        mesh=mesh,
        in_specs=(
            P(("groups", "row", "col"), None),
            P(("groups", "row", "col"), None),
            P(("groups", "row", "col")),
        ),
        out_specs=(P(("groups", "row"), "col"), P(("groups", "row"), "col")),
        check_vma=False,
    )
```

```python
import functools

import jax
import jax.numpy as jnp
from jax import lax
from jax.experimental import pallas as pl
from jax.experimental.pallas import tpu as pltpu
from jax.sharding import PartitionSpec as P


SLOTS, CHUNK, PIECE = 4, 256, 128


def chip_ring(rows):
    width = 2 if rows <= 8 else 4
    depth = rows // width
    order = [z * width for z in range(depth)]
    for step, z in enumerate(reversed(range(depth))):
        columns = range(1, width) if step % 2 == 0 else range(width - 1, 0, -1)
        order += [z * width + x for x in columns]
    return order


def gram_kernel(scale, left_ref, *refs):
    right_refs, out_ref, turned = refs[:-2], refs[-2], refs[-1]

    @pl.when(pl.program_id(0) == 0)
    def _():
        turned[...] = left_ref[...].T

    right = jnp.concatenate([ref[...] for ref in right_refs], axis=0)
    out_ref[...] = jnp.dot(turned[...], right, preferred_element_type=jnp.float32) * scale


def gram(left, rights, scale, steps, tile):
    tokens, height = left.shape
    return pl.pallas_call(
        functools.partial(gram_kernel, scale),
        grid=(steps,),
        in_specs=[pl.BlockSpec((tokens, height), lambda j: (0, 0))]
        + [pl.BlockSpec((part.shape[0], tile), lambda j: (0, j)) for part in rights],
        out_specs=pl.BlockSpec((height, tile), lambda j: (0, j)),
        out_shape=jax.ShapeDtypeStruct((height, steps * tile), jnp.float32),
        scratch_shapes=[pltpu.VMEM((height, tokens), jnp.bfloat16)],
        compiler_params=pltpu.CompilerParams(vmem_limit_bytes=32 * 1024 * 1024),
    )(left, *rights)


def tiles_kernel(scale, groups, ready, lists, outs, aliased, *refs):
    left_refs, refs = refs[: len(ready)], refs[len(ready) :]
    sources = []
    for shards in lists:
        sources.append(refs[:shards])
        refs = refs[shards:]
    refs = refs[aliased:]
    out_refs, turned = refs[:outs], list(refs[outs:-3])
    joined, buffer, sems = refs[-3:]
    turned = [left_ref if done else turned.pop(0) for left_ref, done in zip(left_refs, ready)]

    def copy(group, slot, j, down=0, rows=None):
        _, height, (_, _, _, width), which, row, column, stride, _ = group
        rows = rows or height
        return pltpu.make_async_copy(
            buffer.at[slot, pl.ds(down, rows), pl.ds(0, width)],
            out_refs[which].at[pl.ds(row + down, rows), pl.ds(pl.multiple_of(column + j * stride, 128), width)],
            sems.at[slot],
        )

    done = [index for index, is_ready in enumerate(ready) if is_ready]
    banks = buffer.shape[0] // SLOTS
    for number, group in enumerate(groups):
        left = group[0]
        if left not in done:
            done.append(left)
            turned[left][...] = left_refs[left][...].T
        earlier = groups[number - banks] if number >= banks else None

        def step(j, carry, group=group, earlier=earlier, bank=number % banks):
            left, height, (source, first, apart, width), _, _, _, _, _ = group
            slot = bank * SLOTS + j
            here = pl.ds(pl.multiple_of(first + j * apart, 128), width)
            joined[:, :width] = jnp.concatenate([ref[:, here] for ref in sources[source]], axis=0)
            if earlier is not None:
                copy(earlier, slot, j).wait()
            for down in range(0, height, CHUNK):
                for across in range(0, width, 256):
                    right = joined[:, across : across + 256]
                    for at in range(down, down + CHUNK, PIECE):
                        rows = turned[left][at : at + PIECE, :]
                        product = jnp.dot(rows, right, preferred_element_type=jnp.float32)
                        buffer[slot, at : at + PIECE, across : across + 256] = product * scale
                copy(group, slot, j, down, CHUNK).start()
            return carry

        lax.fori_loop(0, SLOTS, step, 0)
    for number in range(max(0, len(groups) - banks), len(groups)):
        for j in range(SLOTS):
            copy(groups[number], number % banks * SLOTS + j, j).wait()


def tiles(scale, groups, lefts, lists, out_shapes, out=None, ready=(), hand_on=False, banks=1):
    ready = tuple(ready) or (False,) * len(lefts)
    tokens = lists[0][0].shape[0] * len(lists[0])
    whole, anywhere = pl.BlockSpec(memory_space=pltpu.VMEM), pl.BlockSpec(memory_space=pl.ANY)
    operands = [*lefts, *[part for parts in lists for part in parts]]
    specs, aliases = [whole] * len(operands), {}
    if out is not None:
        aliases = {len(operands): 0}
        operands.append(out)
        specs.append(anywhere)
    area = sum(g[1] * g[2][3] * g[7] for g in groups)
    turned = [(left.shape[1], tokens) for left, done in zip(lefts, ready) if not done]
    results = [jax.ShapeDtypeStruct(shape, jnp.float32) for shape in out_shapes]
    result_specs = [anywhere] * len(results)
    if hand_on:
        results.append(pltpu.VMEM(turned[0], jnp.bfloat16))
        result_specs.append(whole)
    return pl.pallas_call(
        functools.partial(
            tiles_kernel, scale, groups, ready, [len(parts) for parts in lists], len(out_shapes), len(aliases)
        ),
        in_specs=specs,
        out_specs=result_specs,
        out_shape=results,
        scratch_shapes=[pltpu.VMEM(shape, jnp.bfloat16) for shape in turned[int(hand_on) :]]
        + [
            pltpu.VMEM((tokens, max(g[2][3] for g in groups)), jnp.bfloat16),
            pltpu.VMEM((banks * SLOTS, max(g[1] for g in groups), max(g[2][3] for g in groups)), jnp.float32),
            pltpu.SemaphoreType.DMA((banks * SLOTS,)),
        ],
        input_output_aliases=aliases,
        compiler_params=pltpu.CompilerParams(vmem_limit_bytes=32 * 1024 * 1024),
        cost_estimate=pl.CostEstimate(flops=2 * tokens * area, bytes_accessed=4 * area, transcendentals=0),
    )(*operands)


def split_kernel(halves, layouts, half_ref, count_ref, act_ref, grad_ref, *out_refs):
    slots = act_ref.shape[0]
    live = lax.broadcasted_iota(jnp.int32, (slots, 128), 0) < count_ref[0]
    for half in range(halves):
        for flip in (1, 0):

            @pl.when((half_ref[0] + flip) % halves == half)
            def _(half=half, flip=flip):
                for chain, layout in enumerate(layouts):
                    target = 0
                    for source, start, width in layout:
                        ref = (grad_ref, act_ref)[source]
                        first = half * (ref.shape[1] // halves) + start
                        values = ref[:, first : first + width]
                        mask = jnp.concatenate([live] * (width // 128), axis=1)
                        masked = jnp.where(mask, values, jnp.zeros_like(values))
                        own = (half + flip) % halves * slots
                        out_ref, columns = out_refs[2 * chain + flip], slice(target, target + width)
                        out_ref[own : own + slots, columns] = masked
                        other = slots - own
                        out_ref[other : other + slots, columns] = jnp.zeros_like(values)
                        target += width


def solution(mesh):
    rows, cols = mesh.shape["row"], mesh.shape["col"]
    order = chip_ring(rows)
    ahead = [(order[p], order[(p + 1) % rows]) for p in range(rows)]
    behind = [(target, source) for source, target in ahead]
    swap = [(0, 1), (1, 0)]
    half_rows = rows // cols
    scale = 1.0 / (9.0 * rows * cols)

    def local(activations, pseudo_grads, row_counts):
        row, col = lax.axis_index("row"), lax.axis_index("col")
        slots, act_width = activations.shape
        grad_width = pseudo_grads.shape[1]
        act_half, grad_half = act_width // cols, grad_width // cols
        act_block, grad_block = act_width // rows, grad_width // rows
        cut = act_block * 4 // 7 if act_block % 1792 == 0 and half_rows == SLOTS else act_block
        rest = act_block - cut
        widths = [half_rows * cut, half_rows * rest + grad_half]
        if rest == 0:
            layouts = [[(1, 0, act_half)], [(0, 0, grad_half)]]
        else:
            layouts = [
                [(1, j * act_block, cut) for j in range(half_rows)],
                [(1, j * act_block + cut, rest) for j in range(half_rows)] + [(0, 0, grad_half)],
            ]
        pieces = pl.pallas_call(
            functools.partial(split_kernel, cols, layouts),
            in_specs=[pl.BlockSpec(memory_space=pltpu.SMEM)] * 2 + [pl.BlockSpec(memory_space=pltpu.VMEM)] * 2,
            out_specs=[pl.BlockSpec(memory_space=pltpu.VMEM)] * 4,
            out_shape=[pltpu.VMEM((2 * slots, width), jnp.bfloat16) for width in widths for _ in (0, 1)],
        )(col[None], row_counts, activations, pseudo_grads)
        chains = [[pieces[2 * k] + lax.ppermute(pieces[2 * k + 1], "col", swap)] for k in (0, 1)]
        forward = [chain[0] for chain in chains]
        backward = list(forward)
        steps, halfway = [0] * len(chains), rows // 2
        sequence = [0, 1] * halfway
        def left_part(chain, pieces, hold=None):
            own = []
            for part in chain:
                cuts = [
                    lax.dynamic_slice_in_dim(part, base + (row % half_rows) * size, size, 1) for base, size in pieces
                ]
                own.append(cuts[0] if len(cuts) == 1 else jnp.concatenate(cuts, axis=1))
            groups = [jnp.concatenate(own[:-1], axis=0), own[-1]]
            mine = col == row // half_rows
            if hold is not None:
                hold.append(groups[1])
            return jnp.concatenate([jnp.where(mine, g, lax.ppermute(g, "col", swap)) for g in groups], axis=0)

        previous, hold, left_first = (), [], None
        for k in sequence:
            chain, middle = chains[k], widths[k] // 2
            steps[k] += 1
            final = steps[k] == halfway
            ahead_of, _ = lax.optimization_barrier((forward[k], previous))
            behind_of, _ = lax.optimization_barrier((backward[k], (previous, hold)))
            previous = forward[k]
            if final:
                ahead_of, behind_of = ahead_of[:, :middle], behind_of[:, middle:]
            forward[k] = lax.ppermute(ahead_of, "row", ahead)
            backward[k] = lax.ppermute(behind_of, "row", behind)
            if not final:
                chain += [forward[k], backward[k]]
                latest = (forward[k], backward[k])
            elif k == 0:
                last_first, _ = lax.optimization_barrier(((forward[k], backward[k]), latest))
                chain.append(jnp.concatenate(last_first, axis=1))
                left_first = left_part(chain, [(0, cut)], hold)

        act_shape, grad_shape = (act_block, act_half), (grad_block, grad_half)
        if rest == 0:
            chains[1].append(jnp.concatenate((forward[1], backward[1]), axis=1))
            left_grad = left_part(chains[1], [(0, grad_block)])
            act_cov = gram(left_first, chains[0], scale, act_half // 256, 256)
            grad_cov = gram(left_grad, chains[1], scale, grad_half // 256, 256)
        else:
            grad_first = half_rows * rest
            first_part, second_part = (0, 0, cut, cut), (1, 0, rest, rest)
            grad_part = (1, grad_first, grad_block, grad_block)

            def square(part, lefts, out, **more):
                at = part * cut // 2
                group = (0, cut, (0, at, cut, cut // 2), 0, 0, at, act_block, half_rows)
                return tiles(scale, [group], lefts, [chains[0]], [act_shape], out, **more)

            act_cov, turned_first = square(0, [left_first], None, hand_on=True)
            last_second, act_cov = lax.optimization_barrier(((forward[1], backward[1]), act_cov))
            chains[1].append(jnp.concatenate(last_second, axis=1))
            left_second = left_part(chains[1], [(0, rest), (grad_first, grad_block)])
            (act_cov,) = square(1, [turned_first], act_cov, ready=[True])
            act_cov, grad_cov = tiles(
                scale,
                [
                    (2, grad_block, grad_part, 1, 0, 0, grad_block, half_rows),
                    (0, cut, second_part, 0, 0, cut, act_block, half_rows),
                    (1, rest, first_part, 0, cut, 0, act_block, half_rows),
                    (1, rest, second_part, 0, cut, cut, act_block, half_rows),
                ],
                [turned_first, left_second[:, :rest], left_second[:, rest:]],
                chains, [act_shape, grad_shape], act_cov, ready=[True, False, False],
            )
        return act_cov, grad_cov

    return jax.shard_map(
        local,
        mesh=mesh,
        in_specs=(
            P(("groups", "row", "col"), None),
            P(("groups", "row", "col"), None),
            P(("groups", "row", "col")),
        ),
        out_specs=(P(("groups", "row"), "col"), P(("groups", "row"), "col")),
        check_vma=False,
    )
```
